128 devices in a mesh: grp: 16 (over y, x), voc: 8 (over z, core).
Axes of the slice: x: 4, y: 4, z: 4, core: 2. Of those that a mesh axis runs over, the one named last changes fastest.
Arguments:
- teacher_rows: bfloat16 [512, 4096], P(('grp', 'voc')), may hold values from -125 to 125
- student_rows: bfloat16 [512, 4096], P(('grp', 'voc')), may hold values from -125 to 125
- teacher_head: bfloat16 [4096, 98304], P(None, ('grp', 'voc')), may hold values from -4 to 4
- student_head: bfloat16 [4096, 98304], P(None, ('grp', 'voc')), may hold values from -4 to 4
- response_ids: int32 [512], replicated, may hold values from 0 to 98303
- lengths: int32 [4], replicated, may hold values from 1 to 128, 384 in all
- seq_order: int32 [4], replicated, may hold values from 0 to 3, each once
Outputs:
- token_kl: float32 [512], P(('grp', 'voc'))
- sampled_gap: float32 [512], P(('grp', 'voc'))
- head_grad: bfloat16 [4096, 98304], P(None, ('grp', 'voc'))
- hidden_grad: bfloat16 [512, 4096], P(('grp', 'voc'))
The draws below stay inside these ranges and needn't reach their ends.
Inputs may be any that keep to these rules, and one draw needn't show every extreme that they name: The lengths sum to exactly 384.
All inputs are finite; a program needn't handle non-finite values.
Results may differ from the reference program's by a relative error of at most 0.017.
Values may be sent and summed in bfloat16 or wider, within the bound.
No kernel may reach another device: no remote copies, remote signals or barrier semaphores. Data moves between devices by JAX's collectives and lax.ppermute only.
A program may use at most 128 MiB of HBM per device.

```python
import math
import jax
import jax.numpy as jnp
import numpy as np

D = 4096
VOCAB = 98304
SEQS = 4
RESP = 128
TOKENS = 512
LIVE = 384


def make_head(key, salt):
    key = jax.random.fold_in(key, salt)
    first = jax.random.fold_in(key, 0)
    scale = 3.0 / math.sqrt(D)
    weights = jnp.clip(jax.random.normal(first, (D, VOCAB), jnp.float32), -6.0, 6.0) * scale
    return weights.astype(jnp.bfloat16)


def make_rows(key, salt):
    key = jax.random.fold_in(key, salt)
    first = jax.random.fold_in(key, 0)
    rows = jnp.clip(jax.random.normal(first, (TOKENS, D), jnp.float32), -6.0, 6.0)
    return rows.astype(jnp.bfloat16)


def draw_teacher_head(key, part):
    return make_head(key, 11)


def draw_student_head(key, part):
    return make_head(key, 12)


def draw_teacher_rows(key, part):
    return make_rows(key, 13)


def draw_student_rows(key, part):
    return make_rows(key, 14)


def set_ends(values, rng, least, largest):
    place = [jax.random.randint(jax.random.fold_in(rng, axis), (), 0, length) for axis, length in enumerate(values.shape)]
    widest = values.shape.index(max(values.shape))
    beside = place[:widest] + [(place[widest] + 1) % values.shape[widest]] + place[widest + 1:]
    return values.at[tuple(place)].set(least).at[tuple(beside)].set(largest)


def skewed_wide(own_key, extent, count, slope):
    loads = [min(1 << octave, count + 1 - (1 << octave)) * (1 << 20) // math.isqrt((1 << octave) ** slope) + 1 for octave in range((count + 1).bit_length()) if 1 << octave <= count]
    scale = 1 + sum(loads) // (1 << 30)
    listing = np.cumsum(np.array([max(1, weight // scale) for weight in loads]))
    pick = jax.random.randint(jax.random.fold_in(own_key, 1), extent, 0, int(listing[len(loads) - 1]))
    start = jnp.left_shift(1, jnp.searchsorted(jnp.asarray(listing, jnp.int32), pick, side="right").astype(jnp.int32))
    grade = start - 1 + jax.random.randint(jax.random.fold_in(own_key, 4), extent, 0, 1 << 30) % jnp.minimum(start, count + 1 - start)
    return jax.random.permutation(jax.random.fold_in(own_key, 2), count)[grade].astype(jnp.int32)


def length_profile(number_of, total, reach, lean):
    loads = [(1 << 20) // math.isqrt(grade ** lean) + 1 for grade in range(2, number_of + 1)]
    surplus, counts = total - reach - (number_of - 1), [1] * (number_of - 1)
    while surplus > 0:
        candidates = [i for i in range(number_of - 1) if counts[i] < reach]
        pool, remaining = sum([loads[i] for i in candidates]), surplus
        for i in candidates:
            more = min(reach - counts[i], max(1, remaining * loads[i] // pool), surplus)
            counts[i] = counts[i] + more
            surplus = surplus - more
    return np.array([reach] + counts)


def ragged_sizes(stream_key, amount, total, bound, lean):
    if amount == 2:
        one = jax.random.randint(stream_key, (), max(1, total - bound), min(bound, total - 1) + 1)
        return jnp.stack([one, total - one])
    sizes = jnp.asarray(length_profile(amount, total, bound, lean), jnp.int32)
    twos = (amount - 1) // 2
    source_of, sink = sizes[1:1 + 2 * twos:2], sizes[2:2 + 2 * twos:2]
    slack = jnp.minimum(source_of - 1, bound - sink)
    moved = jax.random.randint(jax.random.fold_in(stream_key, 1), (twos,), 0, 1 << 20) % (slack + 1)
    sizes = sizes.at[1:1 + 2 * twos:2].set(source_of - moved).at[2:2 + 2 * twos:2].set(sink + moved)
    return sizes[jax.random.permutation(jax.random.fold_in(stream_key, 2), amount)]


def setup_inputs(seed: int = 0) -> dict:
    arg_keys = jax.random.split(jax.random.key(seed), 8)
    return {
        "teacher_rows": draw_teacher_rows(jax.random.fold_in(arg_keys[7], 71), 0),
        "student_rows": draw_student_rows(jax.random.fold_in(arg_keys[7], 71), 0),
        "teacher_head": draw_teacher_head(jax.random.fold_in(arg_keys[7], 71), 0),
        "student_head": draw_student_head(jax.random.fold_in(arg_keys[7], 71), 0),
        "response_ids": set_ends(skewed_wide(arg_keys[4], (TOKENS,), VOCAB, 2), jax.random.fold_in(arg_keys[4], 3), 0, VOCAB - 1).astype(jnp.int32),
        "lengths": ragged_sizes(arg_keys[5], SEQS, LIVE, RESP, 2).astype(jnp.int32),
        "seq_order": jax.random.permutation(arg_keys[6], SEQS).astype(jnp.int32),
    }


def reference(teacher_rows, student_rows, teacher_head, student_head, response_ids, lengths, seq_order):
    aligned = teacher_rows.reshape(SEQS, RESP, D)[seq_order].reshape(TOKENS, D)
    live = (jnp.arange(RESP, dtype=jnp.int32)[None, :] < lengths[:, None]).reshape(TOKENS).astype(jnp.float32)
    student_logits = jnp.dot(student_rows, student_head, preferred_element_type=jnp.float32)
    teacher_logits = jnp.dot(aligned, teacher_head, preferred_element_type=jnp.float32)
    student_lse = jax.nn.logsumexp(student_logits, axis=1)
    teacher_lse = jax.nn.logsumexp(teacher_logits, axis=1)
    spread = student_logits - teacher_logits
    probs = jnp.exp(student_logits - student_lse[:, None])
    average = jnp.sum(probs * spread, axis=1)
    token_kl = live * (average - student_lse + teacher_lse)
    hit = jnp.take_along_axis(spread, response_ids[:, None].astype(jnp.int32), axis=1)[:, 0]
    sampled_gap = live * (hit - student_lse + teacher_lse)
    logit_grad = ((64.0 * live)[:, None] * probs * (spread - average[:, None])).astype(jnp.bfloat16)
    head_grad = jnp.dot(student_rows.T, logit_grad, preferred_element_type=jnp.float32).astype(jnp.bfloat16)
    hidden_grad = jnp.dot(logit_grad, student_head.T, preferred_element_type=jnp.float32).astype(jnp.bfloat16)
    return token_kl, sampled_gap, head_grad, hidden_grad
```

```python
import jax
import jax.numpy as jnp
from jax import lax
from jax.experimental import pallas as pl
from jax.experimental.pallas import tpu as pltpu
from jax.sharding import PartitionSpec as P

AXES = ("grp", "voc")
LOSS_SCALE = 64.0
SIDE = 4
CHIPS = SIDE**3
VMEM_LIMIT = 56 * 1024 * 1024
f32 = jnp.float32
bf16 = jnp.bfloat16


def at(y, x, z, c):
    return ((y * SIDE + x) * SIDE + z) * 2 + c


RANGE = range(SIDE)
PLANES = [[at(y, x, z, 0) for x in RANGE for z in RANGE] for y in RANGE] + [
    [at(y, x, z, 1) for y in RANGE for z in RANGE] for x in RANGE
]
CORES = [[2 * chip + c for chip in range(CHIPS)] for c in range(2)]
SWAP = [(i, i ^ 1) for i in range(2 * CHIPS)]
STEPS = (0, 1, 3, 2)


def along(step):
    pairs = []
    for y in RANGE:
        for x in RANGE:
            for z in RANGE:
                pairs.append((at(y, x, z, 0), at((y - step) % SIDE, x, z, 0)))
                pairs.append((at(y, x, z, 1), at(y, (x - step) % SIDE, z, 1)))
    return pairs


def swap(value):
    return lax.ppermute(value, AXES, SWAP)


def gather_chips(shard):
    wide = jnp.broadcast_to(shard[None], (SIDE * SIDE,) + shard.shape).reshape(-1, shard.shape[1])
    plane = lax.all_to_all(wide, AXES, 0, 0, axis_index_groups=PLANES, tiled=True)
    own = [plane] + [lax.ppermute(plane, AXES, along(step)) for step in STEPS[1:]]
    return own + [swap(piece) for piece in own]


def load_rows(meta, pieces, rows, sems):
    y, x, c = meta[0], meta[1], meta[2]
    half = pieces[0].shape[1]
    copies = []
    for index, piece in enumerate(pieces):
        step = STEPS[index % SIDE]
        kind = c if index < SIDE else 1 - c
        for p in range(SIDE):
            row = jnp.where(kind == 0, (y + step) % SIDE, p)
            col = jnp.where(kind == 0, p, (x + step) % SIDE)
            row = meta[4 + row]
            start = pl.multiple_of((row * SIDE + col) * 32, 32)
            lane = pl.multiple_of(kind * half, half)
            copies.append(
                pltpu.make_async_copy(
                    piece.at[pl.ds(32 * p, 32), :],
                    rows.at[pl.ds(start, 32), pl.ds(lane, half)],
                    sems.at[index * SIDE + p],
                )
            )
    for copy in copies:
        copy.start()
    for copy in copies:
        copy.wait()


def student_kernel(meta, *refs):
    pieces, (head, logits, rows, sems) = refs[:8], refs[8:]

    @pl.when(pl.program_id(0) == 0)
    def _():
        load_rows(meta, pieces, rows, sems)

    logits[...] = jnp.dot(rows[...], head[...], preferred_element_type=f32)


def teacher_kernel(meta, *refs):
    pieces, (head, student, ids, scaled, spread, stats, rows, teacher, table, sems) = refs[:8], refs[8:]
    n = pl.program_id(0)
    total, width = student.shape
    tile = head.shape[1]

    @pl.when(n == 0)
    def _():
        load_rows(meta, pieces, rows, sems)

    teacher[:, pl.ds(pl.multiple_of(n * tile, tile), tile)] = jnp.dot(
        rows[...], head[...], preferred_element_type=f32
    )

    @pl.when(n == pl.num_programs(0) - 1)
    def _():
        chunk = 64
        first = meta[3]

        @pl.loop(0, total // chunk)
        def _(i):
            here = pl.ds(pl.multiple_of(i * chunk, chunk), chunk)
            s, t = student[here, :], teacher[here, :]
            gap = s - t
            top_s = jnp.max(s, axis=1, keepdims=True)
            top_t = jnp.max(t, axis=1, keepdims=True)
            e = jnp.exp(s - top_s)
            column = first + lax.broadcasted_iota(jnp.int32, (chunk, width), 1)
            values = (
                top_s,
                jnp.sum(e, axis=1, keepdims=True),
                jnp.sum(e * gap, axis=1, keepdims=True),
                top_t,
                jnp.sum(jnp.exp(t - top_t), axis=1, keepdims=True),
                jnp.sum(jnp.where(column == ids[here, :], gap, 0.0), axis=1, keepdims=True),
            )
            scaled[here, :] = e
            spread[here, :] = gap
            lane = lax.broadcasted_iota(jnp.int32, (chunk, 128), 1)
            packed = jnp.zeros((chunk, 128), f32)
            for k, value in enumerate(values):
                packed = jnp.where(lane == k, value, packed)
            table[here, :] = packed

        stats[...] = table[...].T[:8]


def grad_kernel(meta, scaled, spread, stats, gathered, head, grad, hidden):
    total = scaled.shape[0]

    @pl.when(pl.program_id(0) == 0)
    def _():
        tops = gathered[:, 0:total]
        top = jnp.max(tops, axis=0, keepdims=True)
        factor = jnp.exp(tops - top)
        sums = jnp.sum(gathered[:, total : 2 * total] * factor, axis=0, keepdims=True)
        moment = jnp.sum(gathered[:, 2 * total : 3 * total] * factor, axis=0, keepdims=True)
        lse = top + jnp.log(sums)
        token = lax.broadcasted_iota(jnp.int32, (1, total), 1)
        live = jnp.zeros((1, total), f32)
        span = total // 4
        for k in range(4):
            inside = (token >= k * span) & (token < k * span + meta[8 + k])
            live = jnp.where(inside, LOSS_SCALE, live)
        weight = live * jnp.exp(stats[0:1, :] - lse)
        average = moment / sums
        line = lax.broadcasted_iota(jnp.int32, (128, total), 0)
        columns = jnp.where(line == 0, weight, jnp.where(line == 1, average, 0.0)).T
        grad[...] = (columns[:, 0:1] * scaled[...] * (spread[...] - columns[:, 1:2])).astype(bf16)

    hidden[...] = lax.dot_general(
        grad[...], head[...], (((1,), (1,)), ((), ())), preferred_element_type=f32
    ).astype(hidden.dtype)


def hidden_kernel(meta, grad, head, hidden):
    hidden[...] = lax.dot_general(
        grad[...], head[...], (((1,), (1,)), ((), ())), preferred_element_type=f32
    ).astype(hidden.dtype)


def params():
    return pltpu.CompilerParams(vmem_limit_bytes=VMEM_LIMIT)


def cost(flops, moved):
    return pl.CostEstimate(flops=flops, bytes_accessed=moved, transcendentals=0)


def logits_call(kernel, meta, pieces, head, extra_in, extra_specs, out_shape, out_specs, scratch):
    depth, width = head.shape
    tile = 256
    anywhere = pl.BlockSpec(memory_space=pl.ANY)
    return pl.pallas_call(
        kernel,
        grid_spec=pltpu.PrefetchScalarGridSpec(
            num_scalar_prefetch=1,
            grid=(width // tile,),
            in_specs=[anywhere] * 8 + [pl.BlockSpec((depth, tile), lambda n, m: (0, n))] + extra_specs,
            out_specs=out_specs,
            scratch_shapes=scratch + [pltpu.SemaphoreType.DMA((32,))],
        ),
        out_shape=out_shape,
        compiler_params=params(),
        cost_estimate=cost(2 * 512 * depth * width, 2 * depth * width + 8 * 512 * 2048),
    )(meta, *pieces, head, *extra_in)


def body(teacher_rows, student_rows, teacher_head, student_head, response_ids, lengths, seq_order):
    depth, width = student_head.shape
    half = depth // 2
    total = response_ids.shape[0]
    own = student_rows.shape[0]
    place = lax.axis_index(AXES)
    c, x, y = place % 2, (place // 8) % SIDE, place // 32

    both = jnp.concatenate([student_rows, teacher_rows], axis=0)
    mine = lax.dynamic_slice_in_dim(both, c * half, half, axis=1)
    theirs = swap(lax.dynamic_slice_in_dim(both, (1 - c) * half, half, axis=1))

    def shard(a, b):
        return jnp.where(c == 0, jnp.concatenate([a, b]), jnp.concatenate([b, a]))

    student_pieces = gather_chips(shard(mine[:own], theirs[:own]))
    teacher_pieces = gather_chips(shard(mine[own:], theirs[own:]))

    position = jnp.arange(4, dtype=jnp.int32)
    inverse = jnp.sum(jnp.where(seq_order[None, :] == position[:, None], position[None, :], 0), axis=1)
    head_meta = jnp.stack([y, x, c, place * width]).astype(jnp.int32)
    student_meta = jnp.concatenate([head_meta, position, lengths])
    teacher_meta = jnp.concatenate([head_meta, inverse, lengths])

    tile = 256
    logits, rows = logits_call(
        student_kernel, student_meta, student_pieces, student_head, [], [],
        [jax.ShapeDtypeStruct((total, width), f32), jax.ShapeDtypeStruct((total, depth), bf16)],
        [pl.BlockSpec((total, tile), lambda n, m: (0, n)), pl.BlockSpec((total, depth), lambda n, m: (0, 0))],
        [],
    )
    fixed = lambda shape: pl.BlockSpec(shape, lambda n, m: (0, 0))
    scaled, spread, stats = logits_call(
        teacher_kernel, teacher_meta, teacher_pieces, teacher_head,
        [logits, response_ids[:, None]], [fixed((total, width)), fixed((total, 1))],
        [
            jax.ShapeDtypeStruct((total, width), f32),
            jax.ShapeDtypeStruct((total, width), f32),
            jax.ShapeDtypeStruct((8, total), f32),
        ],
        [fixed((total, width)), fixed((total, width)), fixed((8, total))],
        [pltpu.VMEM((total, depth), bf16), pltpu.VMEM((total, width), f32), pltpu.VMEM((total, 128), f32)],
    )

    other = swap(stats)
    top_s = jnp.maximum(stats[0], other[0])
    a, b = jnp.exp(stats[0] - top_s), jnp.exp(other[0] - top_s)
    top_t = jnp.maximum(stats[3], other[3])
    chip_t = stats[4] * jnp.exp(stats[3] - top_t) + other[4] * jnp.exp(other[3] - top_t)
    chip_s = jnp.concatenate([top_s, stats[1] * a + other[1] * b, stats[2] * a + other[2] * b])
    chip_t = jnp.stack([top_t, chip_t, stats[5] + other[5]]).reshape(3, CHIPS, 8)
    message = jnp.concatenate(
        [
            jnp.broadcast_to(chip_s[None], (CHIPS, 3 * total)),
            chip_t.transpose(1, 0, 2).reshape(CHIPS, 24),
            jnp.zeros((CHIPS, 104), f32),
        ],
        axis=1,
    )
    gathered = lax.all_to_all(message, AXES, 0, 0, axis_index_groups=CORES, tiled=True)

    block = 512
    count = half // block
    grad, far = pl.pallas_call(
        grad_kernel,
        grid_spec=pltpu.PrefetchScalarGridSpec(
            num_scalar_prefetch=1,
            grid=(count,),
            in_specs=[
                fixed((total, width)),
                fixed((total, width)),
                fixed((8, total)),
                fixed(gathered.shape),
                pl.BlockSpec((block, width), lambda n, m: ((1 - m[2]) * count + n, 0)),
            ],
            out_specs=[fixed((total, width)), pl.BlockSpec((total, block), lambda n, m: (0, n))],
        ),
        out_shape=[
            jax.ShapeDtypeStruct((total, width), bf16),
            jax.ShapeDtypeStruct((total, half), bf16),
        ],
        compiler_params=params(),
        cost_estimate=cost(2 * total * half * width, 12 * total * width + 2 * half * width),
    )(student_meta, scaled, spread, stats, gathered, student_head)
    near = pl.pallas_call(
        hidden_kernel,
        grid_spec=pltpu.PrefetchScalarGridSpec(
            num_scalar_prefetch=1,
            grid=(count,),
            in_specs=[
                fixed((total, width)),
                pl.BlockSpec((block, width), lambda n, m: (m[2] * count + n, 0)),
            ],
            out_specs=pl.BlockSpec((total, block), lambda n, m: (0, n)),
        ),
        out_shape=jax.ShapeDtypeStruct((total, half), f32),
        compiler_params=params(),
        cost_estimate=cost(2 * total * half * width, 4 * total * half + 2 * half * width),
    )(student_meta, grad, student_head)
    chip_sum = (near + swap(far).astype(f32)).astype(bf16)
    parts = lax.all_to_all(chip_sum, AXES, 0, 0, axis_index_groups=CORES, tiled=True)
    head_grad = lax.dot_general(
        rows, grad, (((0,), (0,)), ((), ())), preferred_element_type=f32
    ).astype(bf16)
    mine = jnp.sum(parts.reshape(CHIPS, 8, half).astype(f32), axis=0).astype(bf16)
    keep = lax.dynamic_slice_in_dim(mine, c * own, own)
    take = swap(lax.dynamic_slice_in_dim(mine, (1 - c) * own, own))
    hidden_grad = jnp.where(
        c == 0, jnp.concatenate([keep, take], axis=1), jnp.concatenate([take, keep], axis=1)
    )

    start = place * own
    tokens = lax.dynamic_slice_in_dim(gathered[:, : 3 * total].reshape(CHIPS, 3, total), start, own, axis=2)
    teach = lax.dynamic_slice_in_dim(
        gathered[:, 3 * total : 3 * total + 24].reshape(CHIPS, 3, 8), c * own, own, axis=2
    )
    top = jnp.max(tokens[:, 0], axis=0)
    scale = jnp.exp(tokens[:, 0] - top)
    sums = jnp.sum(tokens[:, 1] * scale, axis=0)
    student_lse = top + jnp.log(sums)
    average = jnp.sum(tokens[:, 2] * scale, axis=0) / sums
    top = jnp.max(teach[:, 0], axis=0)
    teacher_lse = top + jnp.log(jnp.sum(teach[:, 1] * jnp.exp(teach[:, 0] - top), axis=0))
    hit = jnp.sum(teach[:, 2], axis=0)
    span = total // lengths.shape[0]
    index = start + jnp.arange(own, dtype=jnp.int32)
    live = (index % span < lengths[index // span]).astype(f32)
    token_kl = live * (average - student_lse + teacher_lse)
    sampled_gap = live * (hit - student_lse + teacher_lse)
    return (token_kl, sampled_gap, head_grad, hidden_grad)


def solution(mesh):
    in_specs = (P(AXES, None), P(AXES, None), P(None, AXES), P(None, AXES), P(), P(), P())
    out_specs = (P(AXES), P(AXES), P(None, AXES), P(AXES, None))
    return jax.shard_map(body, mesh=mesh, in_specs=in_specs, out_specs=out_specs, check_vma=False)
```

```python
import jax
import jax.numpy as jnp
from jax import lax
from jax.experimental import pallas as pl
from jax.experimental.pallas import tpu as pltpu
from jax.sharding import PartitionSpec as P

AXES = ("grp", "voc")
LOSS_SCALE = 64.0
SIDE = 4
CHIPS = SIDE**3
LARGE, SMALL = 58 * 1024 * 1024, 16 * 1024 * 1024
TILE = 256
TILES = 3
f32 = jnp.float32
bf16 = jnp.bfloat16


def at(y, x, z, c):
    return ((y * SIDE + x) * SIDE + z) * 2 + c


RANGE = range(SIDE)
PLANES = [[at(y, x, z, 0) for x in RANGE for z in RANGE] for y in RANGE] + [
    [at(y, x, z, 1) for y in RANGE for z in RANGE] for x in RANGE
]
CORES = [[2 * chip + c for chip in range(CHIPS)] for c in range(2)]
SWAP = [(i, i ^ 1) for i in range(2 * CHIPS)]
STEPS = (0, 1, 3, 2)


def along(step):
    pairs = []
    for y in RANGE:
        for x in RANGE:
            for z in RANGE:
                pairs.append((at(y, x, z, 0), at((y - step) % SIDE, x, z, 0)))
                pairs.append((at(y, x, z, 1), at(y, (x - step) % SIDE, z, 1)))
    return pairs


def swap(value):
    return lax.ppermute(value, AXES, SWAP)


def assemble(meta, pieces, rows, order):
    y, x, c = meta[0], meta[1], meta[2]
    half = pieces[0].shape[1]
    for index, piece in enumerate(pieces):
        step = STEPS[index % SIDE]
        kind = c if index < SIDE else 1 - c
        for p in range(SIDE):
            row = jnp.where(kind == 0, (y + step) % SIDE, p)
            col = jnp.where(kind == 0, p, (x + step) % SIDE)
            if order is not None:
                row = meta[order + row]
            first = pl.multiple_of((row * SIDE + col) * 32, 32)
            lane = pl.multiple_of(kind * half, half)
            rows[pl.ds(first, 32), pl.ds(lane, half)] = piece[32 * p : 32 * p + 32, :]


def pack(values, rows):
    lane = lax.broadcasted_iota(jnp.int32, (rows, 128), 1)
    packed = jnp.zeros((rows, 128), f32)
    for k, value in enumerate(values):
        packed = jnp.where(lane == k, value, packed)
    return packed


def row_sum(value):
    return jnp.sum(value, axis=1, keepdims=True)


def student_kernel(meta, *refs):
    pieces, (head, logits, scaled, stats, rows, table) = refs[:8], refs[8:]
    n = pl.program_id(0)
    total, width = logits.shape
    tile = head.shape[1]

    @pl.when(n == 0)
    def _():
        assemble(meta, pieces, rows, None)

    logits[:, pl.ds(pl.multiple_of(n * tile, tile), tile)] = jnp.dot(
        rows[...], head[...], preferred_element_type=f32
    )

    @pl.when(n == pl.num_programs(0) - 1)
    def _():
        chunk = 64
        for i in range(total // chunk):
            here = slice(i * chunk, (i + 1) * chunk)
            s = logits[here, :]
            top = jnp.max(s, axis=1, keepdims=True)
            e = jnp.exp(s - top)
            scaled[here, :] = e
            table[here, :] = pack([top, row_sum(e)], chunk)
        stats[...] = table[...].T[:8]


def teacher_kernel(meta, *refs):
    pieces, refs = refs[:8], refs[8:]
    head, student, scaled, ids, stats_s, spread, stats, rows, teacher, moment, hit, tops = refs
    n = pl.program_id(0)
    total, tile = student.shape
    lanes = 128

    @pl.when(n == 0)
    def _():
        assemble(meta, pieces, rows, 4)
        moment[...] = jnp.zeros_like(moment)
        hit[...] = jnp.zeros_like(hit)
        tops[...] = jnp.full_like(tops, -jnp.inf)

    teacher[n] = jnp.dot(rows[...], head[...], preferred_element_type=f32)
    chunk = 64
    for i in range(total // chunk):
        here = slice(i * chunk, (i + 1) * chunk)
        own = ids[here, :] - meta[3] - n * tile
        for part in range(tile // lanes):
            side = slice(part * lanes, (part + 1) * lanes)
            t = teacher[n, here, side]
            gap = student[here, side] - t
            spread[here, side] = gap
            moment[here, :] += scaled[here, side] * gap
            column = part * lanes + lax.broadcasted_iota(jnp.int32, (chunk, lanes), 1)
            hit[here, :] += jnp.where(column == own, gap, 0.0)
            tops[here, :] = jnp.maximum(tops[here, :], t)

    @pl.when(n == pl.num_programs(0) - 1)
    def _():
        for i in range(total // chunk):
            here = slice(i * chunk, (i + 1) * chunk)
            top = jnp.max(tops[here, :], axis=1, keepdims=True)
            sums = jnp.exp(teacher[0, here, :] - top)
            for k in range(1, TILES):
                sums += jnp.exp(teacher[k, here, :] - top)
            moment[here, :] = pack(
                [row_sum(moment[here, :]), top, row_sum(sums), row_sum(hit[here, :])], chunk
            )
        stats[0:2, :] = stats_s[0:2, :]
        stats[2:6, :] = moment[...].T[0:4]
        stats[6:8, :] = jnp.zeros((2, total), f32)


def logits_call(kernel, meta, pieces, head, extra, extra_specs, out_shape, out_specs, scratch):
    total, (depth, width) = 4 * pieces[0].shape[0], head.shape
    once = pl.BlockSpec(pieces[0].shape, lambda n, m: (0, 0), pipeline_mode=pl.Buffered(1))
    return pl.pallas_call(
        kernel,
        grid_spec=pltpu.PrefetchScalarGridSpec(
            num_scalar_prefetch=1,
            grid=(TILES,),
            in_specs=[once] * 8 + [pl.BlockSpec((depth, TILE), lambda n, m: (0, n))] + extra_specs,
            out_specs=out_specs,
            scratch_shapes=scratch,
        ),
        out_shape=out_shape,
        compiler_params=params(LARGE),
        cost_estimate=cost(0, 0),
    )(meta, *pieces, head, *extra)


def turn_kernel(meta, own, far, turned):
    n = pl.program_id(0)
    count = pl.num_programs(0) // 2

    @pl.when(n < count)
    def _():
        turned[...] = own[...].T

    @pl.when(n >= count)
    def _():
        turned[...] = far[...].T


def turn_call(meta, head, far):
    half, width = far.shape
    block = 512
    count = half // block
    return pl.pallas_call(
        turn_kernel,
        grid_spec=pltpu.PrefetchScalarGridSpec(
            num_scalar_prefetch=1,
            grid=(2 * count,),
            in_specs=[
                pl.BlockSpec((block, width), lambda n, m: (m[2] * count + jnp.minimum(n, count - 1), 0)),
                pl.BlockSpec((block, width), lambda n, m: (jnp.maximum(n - count, 0), 0)),
            ],
            out_specs=pl.BlockSpec((width, block), lambda n, m: (n // count, n % count)),
        ),
        out_shape=jax.ShapeDtypeStruct((2 * width, half), bf16),
        compiler_params=params(LARGE),
        cost_estimate=cost(0, 8 * half * width),
    )(meta, head, far)


def grad_kernel(meta, scaled, spread, stats, scaled_o, spread_o, stats_o, gathered, grad):
    total, width = scaled.shape
    tops = gathered[:, 0:total]
    top = jnp.max(tops, axis=0, keepdims=True)
    factor = jnp.exp(tops - top)
    sums = jnp.sum(gathered[:, total : 2 * total] * factor, axis=0, keepdims=True)
    moment = jnp.sum(gathered[:, 2 * total : 3 * total] * factor, axis=0, keepdims=True)
    lse = top + jnp.log(sums)
    token = lax.broadcasted_iota(jnp.int32, (1, total), 1)
    live = jnp.zeros((1, total), f32)
    span = total // 4
    for k in range(4):
        inside = (token >= k * span) & (token < k * span + meta[8 + k])
        live = jnp.where(inside, LOSS_SCALE, live)
    average = moment / sums
    line = lax.broadcasted_iota(jnp.int32, (128, total), 0)
    lines = jnp.where(line == 0, average, 0.0)
    for side, top in enumerate((stats[0:1, :], stats_o[0:1, :])):
        lines = jnp.where(line == side + 1, live * jnp.exp(top - lse), lines)
    columns = lines.T
    for side, (e, gap) in enumerate(((scaled, spread), (scaled_o, spread_o))):
        grad[:, side * width : (side + 1) * width] = (
            columns[:, side + 1 : side + 2] * e[...] * (gap[...] - columns[:, 0:1])
        ).astype(bf16)


def params(limit):
    return pltpu.CompilerParams(vmem_limit_bytes=limit)


def cost(flops, moved):
    return pl.CostEstimate(flops=flops, bytes_accessed=moved, transcendentals=0)


def body(teacher_rows, student_rows, teacher_head, student_head, response_ids, lengths, seq_order):
    depth, width = student_head.shape
    half = depth // 2
    total = response_ids.shape[0]
    own = student_rows.shape[0]
    place = lax.axis_index(AXES)
    c, x, y = place % 2, (place // 8) % SIDE, place // 32

    both = jnp.concatenate([student_rows, teacher_rows], axis=0)
    mine = lax.dynamic_slice_in_dim(both, c * half, half, axis=1)
    theirs = swap(lax.dynamic_slice_in_dim(both, (1 - c) * half, half, axis=1))

    def shard(a, b):
        return jnp.where(c == 0, jnp.concatenate([a, b]), jnp.concatenate([b, a]))

    shards = jnp.stack([shard(mine[:own], theirs[:own]), shard(mine[own:], theirs[own:])])
    wide = jnp.broadcast_to(shards[None], (SIDE * SIDE,) + shards.shape)
    wide = lax.all_to_all(wide, AXES, 0, 0, axis_index_groups=PLANES, tiled=True)

    position = jnp.arange(4, dtype=jnp.int32)
    inverse = jnp.sum(jnp.where(seq_order[None, :] == position[:, None], position[None, :], 0), axis=1)
    meta = jnp.concatenate([jnp.stack([y, x, c, place * width]).astype(jnp.int32), inverse, lengths])
    ids = response_ids[:, None]
    far = lax.dynamic_slice_in_dim(student_head, (1 - c) * half, half)
    wide, meta, ids, far = lax.optimization_barrier((wide, meta, ids, far))
    far = swap(far)

    def along_axis(plane):
        return [plane] + [lax.ppermute(plane, AXES, along(step)) for step in STEPS[1:]]

    student_pieces = along_axis(wide[:, 0].reshape(-1, half))
    teacher_pieces = along_axis(wide[:, 1].reshape(-1, half))
    turned = turn_call(meta, student_head, far)
    student_pieces, turned = lax.optimization_barrier((student_pieces, turned))
    student_pieces += [swap(piece) for piece in student_pieces]

    fixed = lambda shape: pl.BlockSpec(shape, lambda n, m: (0,) * len(shape))
    moving = pl.BlockSpec((total, TILE), lambda n, m: (0, n))
    square = jax.ShapeDtypeStruct((total, width), f32)
    line = jax.ShapeDtypeStruct((8, total), f32)
    logits, scaled, stats_s, rows = logits_call(
        student_kernel, meta, student_pieces, student_head, [], [],
        [square, square, line, jax.ShapeDtypeStruct((total, depth), bf16)],
        [fixed((total, width)), fixed((total, width)), fixed((8, total)), fixed((total, depth))],
        [pltpu.VMEM((total, 128), f32)],
    )
    teacher_pieces, stats_s = lax.optimization_barrier((teacher_pieces, stats_s))
    teacher_pieces += [swap(piece) for piece in teacher_pieces]
    spread, stats = logits_call(
        teacher_kernel, meta, teacher_pieces, teacher_head,
        [logits, scaled, ids, stats_s], [moving, moving, fixed((total, 1)), fixed((8, total))],
        [square, line],
        [moving, fixed((8, total))],
        [pltpu.VMEM((total, depth), bf16), pltpu.VMEM((TILES, total, TILE), f32)]
        + [pltpu.VMEM((total, 128), f32)] * 3,
    )

    other = swap(stats)
    other, scaled, spread = lax.optimization_barrier((other, scaled, spread))
    scaled_o, spread_o = swap(scaled), swap(spread)
    top_s = jnp.maximum(stats[0], other[0])
    a, b = jnp.exp(stats[0] - top_s), jnp.exp(other[0] - top_s)
    top_t = jnp.maximum(stats[3], other[3])
    chip_t = stats[4] * jnp.exp(stats[3] - top_t) + other[4] * jnp.exp(other[3] - top_t)
    chip_s = jnp.concatenate([top_s, stats[1] * a + other[1] * b, stats[2] * a + other[2] * b])
    chip_t = jnp.stack([top_t, chip_t, stats[5] + other[5]]).reshape(3, CHIPS, 8)
    message = jnp.concatenate(
        [
            jnp.broadcast_to(chip_s[None], (CHIPS, 3 * total)),
            chip_t.transpose(1, 0, 2).reshape(CHIPS, 24),
            jnp.zeros((CHIPS, 104), f32),
        ],
        axis=1,
    )
    gathered = lax.all_to_all(message, AXES, 0, 0, axis_index_groups=CORES, tiled=True)

    in_vmem = pl.BlockSpec(memory_space=pltpu.VMEM)
    grad = pl.pallas_call(
        grad_kernel,
        in_specs=[pl.BlockSpec(memory_space=pltpu.SMEM)] + [in_vmem] * 7,
        out_specs=in_vmem,
        out_shape=jax.ShapeDtypeStruct((total, 2 * width), bf16),
        compiler_params=params(SMALL),
        cost_estimate=cost(10 * total * width, 20 * total * width),
    )(meta, scaled, spread, stats, scaled_o, spread_o, other, gathered)
    chip_sum = jnp.dot(grad, turned, preferred_element_type=f32).astype(bf16)
    parts = lax.all_to_all(chip_sum, AXES, 0, 0, axis_index_groups=CORES, tiled=True)
    head_grad = lax.dot_general(
        rows, grad[:, :width], (((0,), (0,)), ((), ())), preferred_element_type=f32
    ).astype(bf16)
    mine = jnp.sum(parts.reshape(CHIPS, 8, half).astype(f32), axis=0).astype(bf16)
    mine, head_grad = lax.optimization_barrier((mine, head_grad))
    keep = lax.dynamic_slice_in_dim(mine, c * own, own)
    take = swap(lax.dynamic_slice_in_dim(mine, (1 - c) * own, own))
    hidden_grad = jnp.where(
        c == 0, jnp.concatenate([keep, take], axis=1), jnp.concatenate([take, keep], axis=1)
    )

    start = place * own
    tokens = lax.dynamic_slice_in_dim(gathered[:, : 3 * total].reshape(CHIPS, 3, total), start, own, axis=2)
    teach = lax.dynamic_slice_in_dim(
        gathered[:, 3 * total : 3 * total + 24].reshape(CHIPS, 3, 8), c * own, own, axis=2
    )
    top = jnp.max(tokens[:, 0], axis=0)
    scale = jnp.exp(tokens[:, 0] - top)
    sums = jnp.sum(tokens[:, 1] * scale, axis=0)
    student_lse = top + jnp.log(sums)
    average = jnp.sum(tokens[:, 2] * scale, axis=0) / sums
    top = jnp.max(teach[:, 0], axis=0)
    teacher_lse = top + jnp.log(jnp.sum(teach[:, 1] * jnp.exp(teach[:, 0] - top), axis=0))
    hit = jnp.sum(teach[:, 2], axis=0)
    span = total // lengths.shape[0]
    index = start + jnp.arange(own, dtype=jnp.int32)
    live = (index % span < lengths[index // span]).astype(f32)
    token_kl = live * (average - student_lse + teacher_lse)
    sampled_gap = live * (hit - student_lse + teacher_lse)
    return (token_kl, sampled_gap, head_grad, hidden_grad)


def solution(mesh):
    in_specs = (P(AXES, None), P(AXES, None), P(None, AXES), P(None, AXES), P(), P(), P())
    out_specs = (P(AXES), P(AXES), P(None, AXES), P(AXES, None))
    return jax.shard_map(body, mesh=mesh, in_specs=in_specs, out_specs=out_specs, check_vma=False)
```

```python
import jax
import jax.numpy as jnp
from jax import lax
from jax.experimental import pallas as pl
from jax.experimental.pallas import tpu as pltpu
from jax.sharding import PartitionSpec as P

AXES = ("grp", "voc")
LOSS_SCALE = 64.0
SIDE = 4
CHIPS = SIDE**3
LARGE, SMALL = 58 * 1024 * 1024, 16 * 1024 * 1024
TILE = 256
TILES = 3
f32 = jnp.float32
bf16 = jnp.bfloat16


def at(y, x, z, c):
    return ((y * SIDE + x) * SIDE + z) * 2 + c


RANGE = range(SIDE)
PLANES = [[at(y, x, z, 0) for x in RANGE for z in RANGE] for y in RANGE] + [
    [at(y, x, z, 1) for y in RANGE for z in RANGE] for x in RANGE
]
CORES = [[2 * chip + c for chip in range(CHIPS)] for c in range(2)]
SWAP = [(i, i ^ 1) for i in range(2 * CHIPS)]
STEPS = (0, 1, 3, 2)


def along(step):
    pairs = []
    for y in RANGE:
        for x in RANGE:
            for z in RANGE:
                pairs.append((at(y, x, z, 0), at((y - step) % SIDE, x, z, 0)))
                pairs.append((at(y, x, z, 1), at(y, (x - step) % SIDE, z, 1)))
    return pairs


def swap(value):
    return lax.ppermute(value, AXES, SWAP)


def assemble(meta, pieces, rows, order):
    y, x, c = meta[0], meta[1], meta[2]
    half = pieces[0].shape[1]
    for index, piece in enumerate(pieces):
        step = STEPS[index % SIDE]
        kind = c if index < SIDE else 1 - c
        for p in range(SIDE):
            row = jnp.where(kind == 0, (y + step) % SIDE, p)
            col = jnp.where(kind == 0, p, (x + step) % SIDE)
            if order is not None:
                row = meta[order + row]
            first = pl.multiple_of((row * SIDE + col) * 32, 32)
            lane = pl.multiple_of(kind * half, half)
            rows[pl.ds(first, 32), pl.ds(lane, half)] = piece[32 * p : 32 * p + 32, :]


def pack(values, rows):
    lane = lax.broadcasted_iota(jnp.int32, (rows, 128), 1)
    packed = jnp.zeros((rows, 128), f32)
    for k, value in enumerate(values):
        packed = jnp.where(lane == k, value, packed)
    return packed


def row_sum(value):
    return jnp.sum(value, axis=1, keepdims=True)


def student_kernel(meta, *refs):
    pieces, (head, logits, scaled, stats, kept, rows, table, sem) = refs[:8], refs[8:]
    n = pl.program_id(0)
    total, width = logits.shape
    tile = head.shape[1]
    save = pltpu.make_async_copy(rows, kept, sem)

    @pl.when(n == 0)
    def _():
        assemble(meta, pieces, rows, None)
        save.start()

    logits[:, pl.ds(pl.multiple_of(n * tile, tile), tile)] = jnp.dot(
        rows[...], head[...], preferred_element_type=f32
    )

    @pl.when(n == pl.num_programs(0) - 1)
    def _():
        chunk = 64
        for i in range(total // chunk):
            here = slice(i * chunk, (i + 1) * chunk)
            s = logits[here, :]
            top = jnp.max(s, axis=1, keepdims=True)
            e = jnp.exp(s - top)
            scaled[here, :] = e
            table[here, :] = pack([top, row_sum(e)], chunk)
        stats[...] = table[...].T[:8]
        save.wait()


def teacher_kernel(meta, *refs):
    pieces, refs = refs[:8], refs[8:]
    head, student, scaled, ids, stats_s, spread, stats, rows, teacher, moment, hit, tops = refs
    n = pl.program_id(0)
    total, tile = student.shape
    lanes = 128

    @pl.when(n == 0)
    def _():
        assemble(meta, pieces, rows, 4)
        moment[...] = jnp.zeros_like(moment)
        hit[...] = jnp.zeros_like(hit)
        tops[...] = jnp.full_like(tops, -jnp.inf)

    teacher[n] = jnp.dot(rows[...], head[...], preferred_element_type=f32)
    chunk = 64
    for i in range(total // chunk):
        here = slice(i * chunk, (i + 1) * chunk)
        own = ids[here, :] - meta[3] - n * tile
        for part in range(tile // lanes):
            side = slice(part * lanes, (part + 1) * lanes)
            t = teacher[n, here, side]
            gap = student[here, side] - t
            spread[here, side] = gap
            moment[here, :] += scaled[here, side] * gap
            column = part * lanes + lax.broadcasted_iota(jnp.int32, (chunk, lanes), 1)
            hit[here, :] += jnp.where(column == own, gap, 0.0)
            tops[here, :] = jnp.maximum(tops[here, :], t)

    @pl.when(n == pl.num_programs(0) - 1)
    def _():
        for i in range(total // chunk):
            here = slice(i * chunk, (i + 1) * chunk)
            top = jnp.max(tops[here, :], axis=1, keepdims=True)
            sums = jnp.exp(teacher[0, here, :] - top)
            for k in range(1, TILES):
                sums += jnp.exp(teacher[k, here, :] - top)
            moment[here, :] = pack(
                [row_sum(moment[here, :]), top, row_sum(sums), row_sum(hit[here, :])], chunk
            )
        moments = moment[...].T
        stats[0:1, :] = stats_s[0:1, :]
        stats[1:2, :] = stats_s[0:1, :] + jnp.log(stats_s[1:2, :])
        stats[2:3, :] = moments[0:1] / stats_s[1:2, :]
        stats[3:4, :] = moments[1:2] + jnp.log(moments[2:3])
        stats[4:5, :] = moments[3:4]
        stats[5:8, :] = jnp.zeros((3, total), f32)


def logits_call(kernel, meta, pieces, head, extra, extra_specs, out_shape, out_specs, scratch):
    total, (depth, width) = 4 * pieces[0].shape[0], head.shape
    once = pl.BlockSpec(pieces[0].shape, lambda n, m: (0, 0), pipeline_mode=pl.Buffered(1))
    return pl.pallas_call(
        kernel,
        grid_spec=pltpu.PrefetchScalarGridSpec(
            num_scalar_prefetch=1,
            grid=(TILES,),
            in_specs=[once] * 8 + [pl.BlockSpec((depth, TILE), lambda n, m: (0, n))] + extra_specs,
            out_specs=out_specs,
            scratch_shapes=scratch,
        ),
        out_shape=out_shape,
        compiler_params=params(LARGE),
        cost_estimate=cost(0, 0),
    )(meta, *pieces, head, *extra)


def turn_kernel(meta, own, far, turned):
    n = pl.program_id(0)
    count = pl.num_programs(0) // 2

    @pl.when(n < count)
    def _():
        turned[...] = own[...].T

    @pl.when(n >= count)
    def _():
        turned[...] = far[...].T


def turn_call(meta, head, far):
    half, width = far.shape
    block = 512
    count = half // block
    return pl.pallas_call(
        turn_kernel,
        grid_spec=pltpu.PrefetchScalarGridSpec(
            num_scalar_prefetch=1,
            grid=(2 * count,),
            in_specs=[
                pl.BlockSpec((block, width), lambda n, m: (m[2] * count + jnp.minimum(n, count - 1), 0)),
                pl.BlockSpec((block, width), lambda n, m: (jnp.maximum(n - count, 0), 0)),
            ],
            out_specs=pl.BlockSpec((width, block), lambda n, m: (n // count, n % count)),
        ),
        out_shape=jax.ShapeDtypeStruct((2 * width, half), bf16),
        compiler_params=params(LARGE),
        cost_estimate=cost(0, 8 * half * width),
    )(meta, head, far)


def chip_lines(own, other):
    a, b = own[1:2, :], other[1:2, :]
    top = jnp.maximum(a, b)
    lse = top + jnp.log(jnp.exp(a - top) + jnp.exp(b - top))
    return lse, own[2:3, :] * jnp.exp(a - lse) + other[2:3, :] * jnp.exp(b - lse)


def stack_lines(values):
    line = lax.broadcasted_iota(jnp.int32, (128, values[0].shape[1]), 0)
    lines = jnp.zeros((128, values[0].shape[1]), f32)
    for k, value in enumerate(values):
        lines = jnp.where(line == k, value, lines)
    return lines


def merge_kernel(own, other, message):
    total = own.shape[1]
    lse, average = chip_lines(own, other)
    for k in range(4):
        here = slice(128 * k, 128 * (k + 1))
        for base, value in ((0, lse), (4, average)):
            lanes = slice(128 * (base + k), 128 * (base + k + 1))
            message[:, :, lanes] = jnp.broadcast_to(value[:, here].reshape(1, 1, 128), (CHIPS, 1, 128))
    a, b = own[3:4, :], other[3:4, :]
    top = jnp.maximum(a, b)
    lse_t = top + jnp.log(jnp.exp(a - top) + jnp.exp(b - top))
    line = lax.broadcasted_iota(jnp.int32, (128, total), 0) % 16
    hit = own[4:5, :] + other[4:5, :]
    values = jnp.where(line == 0, lse_t, jnp.where(line == 1, hit, 0.0)).T
    lane = lax.broadcasted_iota(jnp.int32, (total, 128), 1) // 16
    token = lax.broadcasted_iota(jnp.int32, (total, 128), 0) % 8
    values = jnp.where(lane == token, values, 0.0)
    message[:, :, 1024:1152] = jnp.sum(values.reshape(CHIPS, 8, 128), axis=1, keepdims=True)


def slab_places(meta):
    y, x, c = meta[0], meta[1], meta[2]
    places = []
    for slab in range(SIDE * SIDE):
        row, col = slab // SIDE, slab % SIDE
        step = jnp.where(c == 0, (row - y) % SIDE, (col - x) % SIDE)
        places.append(pl.multiple_of(32 * (SIDE * step + jnp.where(c == 0, col, row)), 32))
    return places


def grad_kernel(meta, scaled, spread, scaled_o, spread_o, stats, stats_o, gathered, grad, pair, merged):
    total, width = grad.shape
    lse, average, live = [], [], []
    token = lax.broadcasted_iota(jnp.int32, (1, 128), 1)
    for k in range(4):
        parts = gathered[:, 0, 128 * k : 128 * (k + 1)]
        top = jnp.max(parts, axis=0, keepdims=True)
        factor = jnp.exp(parts - top)
        sums = jnp.sum(factor, axis=0, keepdims=True)
        lse.append(top + jnp.log(sums))
        moment = gathered[:, 0, 512 + 128 * k : 640 + 128 * k] * factor
        average.append(jnp.sum(moment, axis=0, keepdims=True) / sums)
        live.append(jnp.where(token < meta[8 + k], LOSS_SCALE, 0.0))
    lse, average, live = (jnp.concatenate(value, axis=1) for value in (lse, average, live))
    own, far = (live * jnp.exp(top - lse) for top in (stats[0:1, :], stats_o[0:1, :]))
    lines = stack_lines([average, own, far, lse])
    merged[...] = lines[0:8]
    columns = lines.T
    for slab, first in enumerate(slab_places(meta)):
        rows = slice(32 * slab, 32 * slab + 32)
        for side, (e, gap) in enumerate(((scaled, spread), (scaled_o, spread_o))):
            value = (
                columns[rows, side + 1 : side + 2] * e[rows, :] * (gap[rows, :] - columns[rows, 0:1])
            ).astype(bf16)
            if side == 0:
                grad[rows, :] = value
            pair[pl.ds(first, 32), side * width : (side + 1) * width] = value


def params(limit):
    return pltpu.CompilerParams(vmem_limit_bytes=limit)


def cost(flops, moved):
    return pl.CostEstimate(flops=flops, bytes_accessed=moved, transcendentals=0)


def body(teacher_rows, student_rows, teacher_head, student_head, response_ids, lengths, seq_order):
    depth, width = student_head.shape
    half = depth // 2
    total = response_ids.shape[0]
    own = student_rows.shape[0]
    place = lax.axis_index(AXES)
    c, x, y = place % 2, (place // 8) % SIDE, place // 32

    both = jnp.concatenate([student_rows, teacher_rows], axis=0)
    mine = lax.dynamic_slice_in_dim(both, c * half, half, axis=1)
    theirs = swap(lax.dynamic_slice_in_dim(both, (1 - c) * half, half, axis=1))

    def shard(a, b):
        return jnp.where(c == 0, jnp.concatenate([a, b]), jnp.concatenate([b, a]))

    shards = jnp.stack([shard(mine[:own], theirs[:own]), shard(mine[own:], theirs[own:])])
    wide = jnp.broadcast_to(shards[None], (SIDE * SIDE,) + shards.shape)
    wide = lax.all_to_all(wide, AXES, 0, 0, axis_index_groups=PLANES, tiled=True)

    position = jnp.arange(4, dtype=jnp.int32)
    inverse = jnp.sum(jnp.where(seq_order[None, :] == position[:, None], position[None, :], 0), axis=1)
    meta = jnp.concatenate([jnp.stack([y, x, c, place * width]).astype(jnp.int32), inverse, lengths])
    ids = response_ids[:, None]
    far = lax.dynamic_slice_in_dim(student_head, (1 - c) * half, half)
    wide, meta, ids, far = lax.optimization_barrier((wide, meta, ids, far))
    far = swap(far)

    def along_axis(plane, relay=False):
        after, before = (lax.ppermute(plane, AXES, along(step)) for step in (1, 3))
        if relay:
            return [plane, after, before, lax.ppermute(after, AXES, along(1))]
        return [plane, after, before, lax.ppermute(plane, AXES, along(2))]

    student_pieces = along_axis(wide[:, 0].reshape(-1, half))
    teacher_pieces = along_axis(wide[:, 1].reshape(-1, half), True)
    turned = turn_call(meta, student_head, far)
    student_pieces, turned = lax.optimization_barrier((student_pieces, turned))
    student_pieces += [swap(piece) for piece in student_pieces]

    fixed = lambda shape: pl.BlockSpec(shape, lambda n, m: (0,) * len(shape))
    moving = pl.BlockSpec((total, TILE), lambda n, m: (0, n))
    square = jax.ShapeDtypeStruct((total, width), f32)
    line = jax.ShapeDtypeStruct((8, total), f32)
    logits, scaled, stats_s, rows = logits_call(
        student_kernel, meta, student_pieces, student_head, [], [],
        [square, square, line, jax.ShapeDtypeStruct((total, depth), bf16)],
        [fixed((total, width)), fixed((total, width)), fixed((8, total)), pl.BlockSpec(memory_space=pl.ANY)],
        [pltpu.VMEM((total, depth), bf16), pltpu.VMEM((total, 128), f32), pltpu.SemaphoreType.DMA],
    )
    teacher_pieces, stats_s = lax.optimization_barrier((teacher_pieces, stats_s))
    teacher_pieces += [swap(piece) for piece in teacher_pieces]
    spread, stats = logits_call(
        teacher_kernel, meta, teacher_pieces, teacher_head,
        [logits, scaled, ids, stats_s], [moving, moving, fixed((total, 1)), fixed((8, total))],
        [square, line],
        [moving, fixed((8, total))],
        [pltpu.VMEM((total, depth), bf16), pltpu.VMEM((TILES, total, TILE), f32)]
        + [pltpu.VMEM((total, 128), f32)] * 3,
    )

    other = swap(stats)
    other, scaled, spread = lax.optimization_barrier((other, scaled, spread))
    scaled_o, spread_o = swap(scaled), swap(spread)
    in_vmem = pl.BlockSpec(memory_space=pltpu.VMEM)
    message = pl.pallas_call(
        merge_kernel,
        in_specs=[in_vmem] * 2,
        out_specs=in_vmem,
        out_shape=jax.ShapeDtypeStruct((CHIPS, 1, 1152), f32),
        compiler_params=params(SMALL),
        cost_estimate=cost(0, 0),
    )(stats, other)
    gathered = lax.all_to_all(message, AXES, 0, 0, axis_index_groups=CORES, tiled=True)

    grad, pair, merged = pl.pallas_call(
        grad_kernel,
        in_specs=[pl.BlockSpec(memory_space=pltpu.SMEM)] + [in_vmem] * 7,
        out_specs=[in_vmem] * 3,
        out_shape=[
            jax.ShapeDtypeStruct((total, width), bf16),
            jax.ShapeDtypeStruct((total, 2 * width), bf16),
            jax.ShapeDtypeStruct((8, total), f32),
        ],
        compiler_params=params(SMALL),
        cost_estimate=cost(10 * total * width, 20 * total * width),
    )(meta, scaled, spread, scaled_o, spread_o, stats, other, gathered)
    gathered, merged = lax.optimization_barrier((gathered, merged))
    blocks = jnp.dot(pair, turned, preferred_element_type=f32).astype(bf16)
    blocks = blocks.reshape(SIDE, total // SIDE, half)
    kept = blocks[0].astype(f32)
    for step in STEPS[:0:-1]:
        kept = kept + lax.ppermute(blocks[step], AXES, along(SIDE - step)).astype(f32)
    parts = lax.all_to_all(kept.astype(bf16), AXES, 0, 0, axis_index_groups=PLANES, tiled=True)
    head_grad = lax.dot_general(
        rows, grad, (((0,), (0,)), ((), ())), preferred_element_type=f32
    ).astype(bf16)
    mine = jnp.sum(parts.reshape(SIDE * SIDE, 8, half).astype(f32), axis=0).astype(bf16)
    mine, head_grad = lax.optimization_barrier((mine, head_grad))
    keep = lax.dynamic_slice_in_dim(mine, c * own, own)
    take = swap(lax.dynamic_slice_in_dim(mine, (1 - c) * own, own))
    hidden_grad = jnp.where(
        c == 0, jnp.concatenate([keep, take], axis=1), jnp.concatenate([take, keep], axis=1)
    )

    start = place * own
    mine = lax.dynamic_slice_in_dim(merged, start, own, axis=1)
    average, student_lse = mine[0], mine[3]
    teach = lax.dynamic_slice_in_dim(gathered[:, 0, 1024:].reshape(CHIPS, 8, 16), c * own, own, axis=1)
    teacher_lse = jax.nn.logsumexp(teach[:, :, 0], axis=0)
    hit = jnp.sum(teach[:, :, 1], axis=0)
    span = total // lengths.shape[0]
    index = start + jnp.arange(own, dtype=jnp.int32)
    live = (index % span < lengths[index // span]).astype(f32)
    token_kl = live * (average - student_lse + teacher_lse)
    sampled_gap = live * (hit - student_lse + teacher_lse)
    return (token_kl, sampled_gap, head_grad, hidden_grad)


def solution(mesh):
    in_specs = (P(AXES, None), P(AXES, None), P(None, AXES), P(None, AXES), P(), P(), P())
    out_specs = (P(AXES), P(AXES), P(None, AXES), P(AXES, None))
    return jax.shard_map(body, mesh=mesh, in_specs=in_specs, out_specs=out_specs, check_vma=False)
```

```python
import jax
import jax.numpy as jnp
from jax import lax
from jax.experimental import pallas as pl
from jax.experimental.pallas import tpu as pltpu
from jax.sharding import PartitionSpec as P

AXES = ("grp", "voc")
LOSS_SCALE = 64.0
SIDE = 4
CHIPS = SIDE**3
LARGE, SMALL = 58 * 1024 * 1024, 16 * 1024 * 1024
TILE = 256
TILES = 3
f32 = jnp.float32
bf16 = jnp.bfloat16


def at(y, x, z, c):
    return ((y * SIDE + x) * SIDE + z) * 2 + c


RANGE = range(SIDE)
PLANES = [[at(y, x, z, 0) for x in RANGE for z in RANGE] for y in RANGE] + [
    [at(y, x, z, 1) for y in RANGE for z in RANGE] for x in RANGE
]
CORES = [[2 * chip + c for chip in range(CHIPS)] for c in range(2)]
SWAP = [(i, i ^ 1) for i in range(2 * CHIPS)]
STEPS = (0, 1, 3, 2)


def along(step):
    pairs = []
    for y in RANGE:
        for x in RANGE:
            for z in RANGE:
                pairs.append((at(y, x, z, 0), at((y - step) % SIDE, x, z, 0)))
                pairs.append((at(y, x, z, 1), at(y, (x - step) % SIDE, z, 1)))
    return pairs


def swap(value):
    return lax.ppermute(value, AXES, SWAP)


def assemble(meta, pieces, rows, order):
    y, x, c = meta[0], meta[1], meta[2]
    half = pieces[0].shape[1]
    for index, piece in enumerate(pieces):
        step = STEPS[index % SIDE]
        kind = c if index < SIDE else 1 - c
        for p in range(SIDE):
            row = jnp.where(kind == 0, (y + step) % SIDE, p)
            col = jnp.where(kind == 0, p, (x + step) % SIDE)
            if order is not None:
                row = meta[order + row]
            first = pl.multiple_of((row * SIDE + col) * 32, 32)
            lane = pl.multiple_of(kind * half, half)
            rows[pl.ds(first, 32), pl.ds(lane, half)] = piece[32 * p : 32 * p + 32, :]


def pack(values, rows):
    lane = lax.broadcasted_iota(jnp.int32, (rows, 128), 1)
    packed = jnp.zeros((rows, 128), f32)
    for k, value in enumerate(values):
        packed = jnp.where(lane == k, value, packed)
    return packed


def row_sum(value):
    return jnp.sum(value, axis=1, keepdims=True)


def student_kernel(meta, *refs):
    pieces, (head, logits, scaled, stats, kept, rows, table, sem) = refs[:8], refs[8:]
    n = pl.program_id(0)
    total, width = logits.shape
    tile = head.shape[1]
    save = pltpu.make_async_copy(rows, kept, sem)

    @pl.when(n == 0)
    def _():
        assemble(meta, pieces, rows, None)
        save.start()

    logits[:, pl.ds(pl.multiple_of(n * tile, tile), tile)] = jnp.dot(
        rows[...], head[...], preferred_element_type=f32
    )

    @pl.when(n == pl.num_programs(0) - 1)
    def _():
        chunk = 64
        for i in range(total // chunk):
            here = slice(i * chunk, (i + 1) * chunk)
            s = logits[here, :]
            top = jnp.max(s, axis=1, keepdims=True)
            e = jnp.exp(s - top)
            scaled[here, :] = e
            table[here, :] = pack([top, row_sum(e)], chunk)
        stats[...] = table[...].T[:8]
        save.wait()


def teacher_kernel(meta, *refs):
    pieces, refs = refs[:8], refs[8:]
    head, student, scaled, ids, stats_s, spread, message, rows, teacher, moment, hit, tops = refs
    n = pl.program_id(0)
    total, tile = student.shape
    lanes = 128

    @pl.when(n == 0)
    def _():
        assemble(meta, pieces, rows, 4)
        moment[...] = jnp.zeros_like(moment)
        hit[...] = jnp.zeros_like(hit)
        tops[...] = jnp.full_like(tops, -jnp.inf)

    teacher[n] = jnp.dot(rows[...], head[...], preferred_element_type=f32)
    chunk = 64
    for i in range(total // chunk):
        here = slice(i * chunk, (i + 1) * chunk)
        own = ids[here, :] - meta[3] - n * tile
        for part in range(tile // lanes):
            side = slice(part * lanes, (part + 1) * lanes)
            t = teacher[n, here, side]
            gap = student[here, side] - t
            spread[here, side] = gap
            moment[here, :] += scaled[here, side] * gap
            column = part * lanes + lax.broadcasted_iota(jnp.int32, (chunk, lanes), 1)
            hit[here, :] += jnp.where(column == own, gap, 0.0)
            tops[here, :] = jnp.maximum(tops[here, :], t)

    @pl.when(n == pl.num_programs(0) - 1)
    def _():
        for i in range(total // chunk):
            here = slice(i * chunk, (i + 1) * chunk)
            top = jnp.max(tops[here, :], axis=1, keepdims=True)
            sums = jnp.exp(teacher[0, here, :] - top)
            for k in range(1, TILES):
                sums += jnp.exp(teacher[k, here, :] - top)
            moment[here, :] = pack(
                [row_sum(moment[here, :]), top, row_sum(sums), row_sum(hit[here, :])], chunk
            )
        moments = moment[...].T
        write_message(
            message,
            stats_s[0:1, :] + jnp.log(stats_s[1:2, :]),
            moments[0:1] / stats_s[1:2, :],
            moments[1:2] + jnp.log(moments[2:3]),
            moments[3:4],
        )


def logits_call(kernel, meta, pieces, head, extra, extra_specs, out_shape, out_specs, scratch):
    total, (depth, width) = 4 * pieces[0].shape[0], head.shape
    once = pl.BlockSpec(pieces[0].shape, lambda n, m: (0, 0), pipeline_mode=pl.Buffered(1))
    return pl.pallas_call(
        kernel,
        grid_spec=pltpu.PrefetchScalarGridSpec(
            num_scalar_prefetch=1,
            grid=(TILES,),
            in_specs=[once] * 8 + [pl.BlockSpec((depth, TILE), lambda n, m: (0, n))] + extra_specs,
            out_specs=out_specs,
            scratch_shapes=scratch,
        ),
        out_shape=out_shape,
        compiler_params=params(LARGE),
        cost_estimate=cost(0, 0),
    )(meta, *pieces, head, *extra)


def turn_kernel(meta, own, far, turned):
    n = pl.program_id(0)
    count = pl.num_programs(0) // 2

    @pl.when(n < count)
    def _():
        turned[...] = own[...].T

    @pl.when(n >= count)
    def _():
        turned[...] = far[...].T


def turn_call(meta, head, far):
    half, width = far.shape
    block = 512
    count = half // block
    return pl.pallas_call(
        turn_kernel,
        grid_spec=pltpu.PrefetchScalarGridSpec(
            num_scalar_prefetch=1,
            grid=(2 * count,),
            in_specs=[
                pl.BlockSpec((block, width), lambda n, m: (m[2] * count + jnp.minimum(n, count - 1), 0)),
                pl.BlockSpec((block, width), lambda n, m: (jnp.maximum(n - count, 0), 0)),
            ],
            out_specs=pl.BlockSpec((width, block), lambda n, m: (n // count, n % count)),
        ),
        out_shape=jax.ShapeDtypeStruct((2 * width, half), bf16),
        compiler_params=params(LARGE),
        cost_estimate=cost(0, 8 * half * width),
    )(meta, head, far)


def stack_lines(values):
    line = lax.broadcasted_iota(jnp.int32, (128, values[0].shape[1]), 0)
    lines = jnp.zeros((128, values[0].shape[1]), f32)
    for k, value in enumerate(values):
        lines = jnp.where(line == k, value, lines)
    return lines


def write_message(message, lse, average, lse_t, hit):
    total = lse.shape[1]
    for k in range(4):
        here = slice(128 * k, 128 * (k + 1))
        for base, value in ((0, lse), (4, average)):
            lanes = slice(128 * (base + k), 128 * (base + k + 1))
            message[:, :, lanes] = jnp.broadcast_to(value[:, here].reshape(1, 1, 128), (CHIPS, 1, 128))
    line = lax.broadcasted_iota(jnp.int32, (128, total), 0) % 16
    values = jnp.where(line == 0, lse_t, jnp.where(line == 1, hit, 0.0)).T
    lane = lax.broadcasted_iota(jnp.int32, (total, 128), 1) // 16
    token = lax.broadcasted_iota(jnp.int32, (total, 128), 0) % 8
    values = jnp.where(lane == token, values, 0.0)
    message[:, :, 1024:1152] = jnp.sum(values.reshape(CHIPS, 8, 128), axis=1, keepdims=True)


def slab_places(meta):
    y, x, c = meta[0], meta[1], meta[2]
    places = []
    for slab in range(SIDE * SIDE):
        row, col = slab // SIDE, slab % SIDE
        step = jnp.where(c == 0, (row - y) % SIDE, (col - x) % SIDE)
        places.append(pl.multiple_of(32 * (SIDE * step + jnp.where(c == 0, col, row)), 32))
    return places


def grad_kernel(
    meta, scaled, spread, scaled_o, spread_o, stats, stats_o, gathered, gathered_o, grad, pair, merged
):
    total, width = grad.shape
    lse, average, live = [], [], []
    token = lax.broadcasted_iota(jnp.int32, (1, 128), 1)
    for k in range(4):
        both = (gathered, gathered_o)
        parts = [part[:, 0, 128 * k : 128 * (k + 1)] for part in both]
        top = jnp.max(jnp.maximum(*parts), axis=0, keepdims=True)
        factors = [jnp.exp(part - top) for part in parts]
        sums = jnp.sum(factors[0] + factors[1], axis=0, keepdims=True)
        lse.append(top + jnp.log(sums))
        moments = [part[:, 0, 512 + 128 * k : 640 + 128 * k] for part in both]
        moment = moments[0] * factors[0] + moments[1] * factors[1]
        average.append(jnp.sum(moment, axis=0, keepdims=True) / sums)
        live.append(jnp.where(token < meta[8 + k], LOSS_SCALE, 0.0))
    lse, average, live = (jnp.concatenate(value, axis=1) for value in (lse, average, live))
    own, far = (live * jnp.exp(top - lse) for top in (stats[0:1, :], stats_o[0:1, :]))
    lines = stack_lines([average, own, far, lse])
    merged[...] = lines[0:8]
    columns = lines.T
    for slab, first in enumerate(slab_places(meta)):
        rows = slice(32 * slab, 32 * slab + 32)
        for side, (e, gap) in enumerate(((scaled, spread), (scaled_o, spread_o))):
            value = (
                columns[rows, side + 1 : side + 2] * e[rows, :] * (gap[rows, :] - columns[rows, 0:1])
            ).astype(bf16)
            if side == 0:
                grad[rows, :] = value
            pair[pl.ds(first, 32), side * width : (side + 1) * width] = value


def params(limit):
    return pltpu.CompilerParams(vmem_limit_bytes=limit)


def cost(flops, moved):
    return pl.CostEstimate(flops=flops, bytes_accessed=moved, transcendentals=0)


def body(teacher_rows, student_rows, teacher_head, student_head, response_ids, lengths, seq_order):
    depth, width = student_head.shape
    half = depth // 2
    total = response_ids.shape[0]
    own = student_rows.shape[0]
    place = lax.axis_index(AXES)
    c, x, y = place % 2, (place // 8) % SIDE, place // 32

    both = jnp.concatenate([student_rows, teacher_rows], axis=0)
    mine = lax.dynamic_slice_in_dim(both, c * half, half, axis=1)
    theirs = swap(lax.dynamic_slice_in_dim(both, (1 - c) * half, half, axis=1))

    def shard(a, b):
        return jnp.where(c == 0, jnp.concatenate([a, b]), jnp.concatenate([b, a]))

    shards = jnp.stack([shard(mine[:own], theirs[:own]), shard(mine[own:], theirs[own:])])
    wide = jnp.broadcast_to(shards[None], (SIDE * SIDE,) + shards.shape)
    wide = lax.all_to_all(wide, AXES, 0, 0, axis_index_groups=PLANES, tiled=True)

    position = jnp.arange(4, dtype=jnp.int32)
    inverse = jnp.sum(jnp.where(seq_order[None, :] == position[:, None], position[None, :], 0), axis=1)
    meta = jnp.concatenate([jnp.stack([y, x, c, place * width]).astype(jnp.int32), inverse, lengths])
    ids = response_ids[:, None]
    far = lax.dynamic_slice_in_dim(student_head, (1 - c) * half, half)
    wide, meta, ids, far = lax.optimization_barrier((wide, meta, ids, far))
    far = swap(far)

    def along_axis(plane, relay=False):
        after, before = (lax.ppermute(plane, AXES, along(step)) for step in (1, 3))
        if relay:
            return [plane, after, before, lax.ppermute(after, AXES, along(1))]
        return [plane, after, before, lax.ppermute(plane, AXES, along(2))]

    student_pieces = along_axis(wide[:, 0].reshape(-1, half))
    teacher_pieces = along_axis(wide[:, 1].reshape(-1, half), True)
    turned = turn_call(meta, student_head, far)
    near = swap(teacher_pieces[0])
    student_pieces, turned, near = lax.optimization_barrier((student_pieces, turned, near))
    student_pieces += [swap(piece) for piece in student_pieces]

    fixed = lambda shape: pl.BlockSpec(shape, lambda n, m: (0,) * len(shape))
    moving = pl.BlockSpec((total, TILE), lambda n, m: (0, n))
    square = jax.ShapeDtypeStruct((total, width), f32)
    line = jax.ShapeDtypeStruct((8, total), f32)
    logits, scaled, stats_s, rows = logits_call(
        student_kernel, meta, student_pieces, student_head, [], [],
        [square, square, line, jax.ShapeDtypeStruct((total, depth), bf16)],
        [fixed((total, width)), fixed((total, width)), fixed((8, total)), pl.BlockSpec(memory_space=pl.ANY)],
        [pltpu.VMEM((total, depth), bf16), pltpu.VMEM((total, 128), f32), pltpu.SemaphoreType.DMA],
    )
    teacher_pieces, stats_s = lax.optimization_barrier((teacher_pieces, stats_s))
    teacher_pieces += [near] + [swap(piece) for piece in teacher_pieces[1:]]
    spread, message = logits_call(
        teacher_kernel, meta, teacher_pieces, teacher_head,
        [logits, scaled, ids, stats_s], [moving, moving, fixed((total, 1)), fixed((8, total))],
        [square, jax.ShapeDtypeStruct((CHIPS, 1, 1152), f32)],
        [moving, fixed((CHIPS, 1, 1152))],
        [pltpu.VMEM((total, depth), bf16), pltpu.VMEM((TILES, total, TILE), f32)]
        + [pltpu.VMEM((total, 128), f32)] * 3,
    )

    gathered = lax.all_to_all(message, AXES, 0, 0, axis_index_groups=CORES, tiled=True)
    scaled_o, spread_o, stats_o = swap(scaled), swap(spread), swap(stats_s)
    gathered_o = swap(gathered)
    in_vmem = pl.BlockSpec(memory_space=pltpu.VMEM)
    grad, pair, merged = pl.pallas_call(
        grad_kernel,
        in_specs=[pl.BlockSpec(memory_space=pltpu.SMEM)] + [in_vmem] * 8,
        out_specs=[in_vmem] * 3,
        out_shape=[
            jax.ShapeDtypeStruct((total, width), bf16),
            jax.ShapeDtypeStruct((total, 2 * width), bf16),
            jax.ShapeDtypeStruct((8, total), f32),
        ],
        compiler_params=params(SMALL),
        cost_estimate=cost(10 * total * width, 20 * total * width),
    )(meta, scaled, spread, scaled_o, spread_o, stats_s, stats_o, gathered, gathered_o)
    gathered, gathered_o, merged = lax.optimization_barrier((gathered, gathered_o, merged))
    blocks = jnp.dot(pair, turned, preferred_element_type=f32).astype(bf16)
    blocks = blocks.reshape(SIDE, total // SIDE, half)
    kept = blocks[0].astype(f32)
    for step in STEPS[:0:-1]:
        kept = kept + lax.ppermute(blocks[step], AXES, along(SIDE - step)).astype(f32)
    parts = lax.all_to_all(kept.astype(bf16), AXES, 0, 0, axis_index_groups=PLANES, tiled=True)
    head_grad = lax.dot_general(
        rows, grad, (((0,), (0,)), ((), ())), preferred_element_type=f32
    ).astype(bf16)
    mine = jnp.sum(parts.reshape(SIDE * SIDE, 8, half).astype(f32), axis=0).astype(bf16)
    mine, head_grad = lax.optimization_barrier((mine, head_grad))
    keep = lax.dynamic_slice_in_dim(mine, c * own, own)
    take = swap(lax.dynamic_slice_in_dim(mine, (1 - c) * own, own))
    hidden_grad = jnp.where(
        c == 0, jnp.concatenate([keep, take], axis=1), jnp.concatenate([take, keep], axis=1)
    )

    start = place * own
    mine = lax.dynamic_slice_in_dim(merged, start, own, axis=1)
    average, student_lse = mine[0], mine[3]
    teach = jnp.concatenate([gathered[:, 0, 1024:], gathered_o[:, 0, 1024:]]).reshape(2 * CHIPS, 8, 16)
    teach = lax.dynamic_slice_in_dim(teach, c * own, own, axis=1)
    teacher_lse = jax.nn.logsumexp(teach[:, :, 0], axis=0)
    hit = jnp.sum(teach[:, :, 1], axis=0)
    span = total // lengths.shape[0]
    index = start + jnp.arange(own, dtype=jnp.int32)
    live = (index % span < lengths[index // span]).astype(f32)
    token_kl = live * (average - student_lse + teacher_lse)
    sampled_gap = live * (hit - student_lse + teacher_lse)
    return (token_kl, sampled_gap, head_grad, hidden_grad)


def solution(mesh):
    in_specs = (P(AXES, None), P(AXES, None), P(None, AXES), P(None, AXES), P(), P(), P())
    out_specs = (P(AXES), P(AXES), P(None, AXES), P(AXES, None))
    return jax.shard_map(body, mesh=mesh, in_specs=in_specs, out_specs=out_specs, check_vma=False)
```

```python
import jax
import jax.numpy as jnp
from jax import lax
from jax.experimental import pallas as pl
from jax.experimental.pallas import tpu as pltpu
from jax.sharding import PartitionSpec as P

AXES = ("grp", "voc")
LOSS_SCALE = 64.0
SIDE = 4
CHIPS = SIDE**3
LARGE, SMALL = 58 * 1024 * 1024, 16 * 1024 * 1024
STUDENT, TEACHER = 47 * 1024 * 1024, 53 * 1024 * 1024
TILE = 256
TILES = 3
f32 = jnp.float32
bf16 = jnp.bfloat16


def at(y, x, z, c):
    return ((y * SIDE + x) * SIDE + z) * 2 + c


RANGE = range(SIDE)
PLANES = [[at(y, x, z, 0) for x in RANGE for z in RANGE] for y in RANGE] + [
    [at(y, x, z, 1) for y in RANGE for z in RANGE] for x in RANGE
]
CORES = [[2 * chip + c for chip in range(CHIPS)] for c in range(2)]
SWAP = [(i, i ^ 1) for i in range(2 * CHIPS)]
STEPS = (0, 1, 3, 2)


def along(step):
    pairs = []
    for y in RANGE:
        for x in RANGE:
            for z in RANGE:
                pairs.append((at(y, x, z, 0), at((y - step) % SIDE, x, z, 0)))
                pairs.append((at(y, x, z, 1), at(y, (x - step) % SIDE, z, 1)))
    return pairs


def swap(value):
    return lax.ppermute(value, AXES, SWAP)


def assemble(meta, pieces, rows, order):
    y, x, c = meta[0], meta[1], meta[2]
    half = pieces[0].shape[1]
    for index, piece in enumerate(pieces):
        step = STEPS[index % SIDE]
        kind = c if index < SIDE else 1 - c
        for p in range(SIDE):
            row = jnp.where(kind == 0, (y + step) % SIDE, p)
            col = jnp.where(kind == 0, p, (x + step) % SIDE)
            if order is not None:
                row = meta[order + row]
            first = pl.multiple_of((row * SIDE + col) * 32, 32)
            lane = pl.multiple_of(kind * half, half)
            rows[pl.ds(first, 32), pl.ds(lane, half)] = piece[32 * p : 32 * p + 32, :]


def pack(values, rows):
    lane = lax.broadcasted_iota(jnp.int32, (rows, 128), 1)
    packed = jnp.zeros((rows, 128), f32)
    for k, value in enumerate(values):
        packed = jnp.where(lane == k, value, packed)
    return packed


def row_sum(value):
    return jnp.sum(value, axis=1, keepdims=True)


def student_kernel(meta, *refs):
    pieces, (head, logits, scaled, stats, kept, rows, table, sem) = refs[:8], refs[8:]
    n = pl.program_id(0)
    total, width = logits.shape
    tile = head.shape[1]
    save = pltpu.make_async_copy(rows, kept, sem)

    @pl.when(n == 0)
    def _():
        assemble(meta, pieces, rows, None)
        save.start()

    logits[:, pl.ds(pl.multiple_of(n * tile, tile), tile)] = jnp.dot(
        rows[...], head[...], preferred_element_type=f32
    )

    @pl.when(n == pl.num_programs(0) - 1)
    def _():
        chunk = 64
        for i in range(total // chunk):
            here = slice(i * chunk, (i + 1) * chunk)
            s = logits[here, :]
            top = jnp.max(s, axis=1, keepdims=True)
            e = jnp.exp(s - top)
            scaled[here, :] = e
            table[here, :] = pack([top, row_sum(e)], chunk)
        stats[...] = table[...].T[:8]
        save.wait()


def teacher_kernel(meta, *refs):
    pieces, refs = refs[:8], refs[8:]
    head, student, scaled, ids, stats_s, spread, message, rows, teacher, moment, hit, tops = refs
    n = pl.program_id(0)
    total, tile = student.shape
    lanes = 128

    @pl.when(n == 0)
    def _():
        assemble(meta, pieces, rows, 4)
        moment[...] = jnp.zeros_like(moment)
        hit[...] = jnp.zeros_like(hit)
        tops[...] = jnp.full_like(tops, -jnp.inf)

    teacher[n] = jnp.dot(rows[...], head[...], preferred_element_type=f32)
    chunk = 64
    for i in range(total // chunk):
        here = slice(i * chunk, (i + 1) * chunk)
        own = ids[here, :] - meta[3] - n * tile
        for part in range(tile // lanes):
            side = slice(part * lanes, (part + 1) * lanes)
            t = teacher[n, here, side]
            gap = student[here, side] - t
            spread[here, side] = gap
            moment[here, :] += scaled[here, side] * gap
            column = part * lanes + lax.broadcasted_iota(jnp.int32, (chunk, lanes), 1)
            hit[here, :] += jnp.where(column == own, gap, 0.0)
            tops[here, :] = jnp.maximum(tops[here, :], t)

    @pl.when(n == pl.num_programs(0) - 1)
    def _():
        for i in range(total // chunk):
            here = slice(i * chunk, (i + 1) * chunk)
            top = jnp.max(tops[here, :], axis=1, keepdims=True)
            sums = jnp.exp(teacher[0, here, :] - top)
            for k in range(1, TILES):
                sums += jnp.exp(teacher[k, here, :] - top)
            moment[here, :] = pack(
                [row_sum(moment[here, :]), top, row_sum(sums), row_sum(hit[here, :])], chunk
            )
        moments = moment[...].T
        write_message(
            message,
            stats_s[0:1, :] + jnp.log(stats_s[1:2, :]),
            moments[0:1] / stats_s[1:2, :],
            moments[1:2] + jnp.log(moments[2:3]),
            moments[3:4],
        )


def logits_call(limit, kernel, meta, pieces, head, extra, extra_specs, out_shape, out_specs, scratch):
    total, (depth, width) = 4 * pieces[0].shape[0], head.shape
    once = pl.BlockSpec(pieces[0].shape, lambda n, m: (0, 0), pipeline_mode=pl.Buffered(1))
    return pl.pallas_call(
        kernel,
        grid_spec=pltpu.PrefetchScalarGridSpec(
            num_scalar_prefetch=1,
            grid=(TILES,),
            in_specs=[once] * 8 + [pl.BlockSpec((depth, TILE), lambda n, m: (0, n))] + extra_specs,
            out_specs=out_specs,
            scratch_shapes=scratch,
        ),
        out_shape=out_shape,
        compiler_params=params(limit),
        cost_estimate=cost(0, 0),
    )(meta, *pieces, head, *extra)


def turn_kernel(meta, own, far, turned):
    n = pl.program_id(0)
    count = pl.num_programs(0) // 2

    @pl.when(n < count)
    def _():
        turned[...] = own[...].T

    @pl.when(n >= count)
    def _():
        turned[...] = far[...].T


def turn_call(meta, head, far):
    half, width = far.shape
    block = 512
    count = half // block
    return pl.pallas_call(
        turn_kernel,
        grid_spec=pltpu.PrefetchScalarGridSpec(
            num_scalar_prefetch=1,
            grid=(2 * count,),
            in_specs=[
                pl.BlockSpec((block, width), lambda n, m: (m[2] * count + jnp.minimum(n, count - 1), 0)),
                pl.BlockSpec((block, width), lambda n, m: (jnp.maximum(n - count, 0), 0)),
            ],
            out_specs=pl.BlockSpec((width, block), lambda n, m: (n // count, n % count)),
        ),
        out_shape=jax.ShapeDtypeStruct((2 * width, half), bf16),
        compiler_params=params(LARGE),
        cost_estimate=cost(0, 8 * half * width),
    )(meta, head, far)


def stack_lines(values):
    line = lax.broadcasted_iota(jnp.int32, (128, values[0].shape[1]), 0)
    lines = jnp.zeros((128, values[0].shape[1]), f32)
    for k, value in enumerate(values):
        lines = jnp.where(line == k, value, lines)
    return lines


def write_message(message, lse, average, lse_t, hit):
    total = lse.shape[1]
    for k in range(4):
        here = slice(128 * k, 128 * (k + 1))
        for base, value in ((0, lse), (4, average)):
            lanes = slice(128 * (base + k), 128 * (base + k + 1))
            message[:, :, lanes] = jnp.broadcast_to(value[:, here].reshape(1, 1, 128), (CHIPS, 1, 128))
    line = lax.broadcasted_iota(jnp.int32, (128, total), 0) % 16
    values = jnp.where(line == 0, lse_t, jnp.where(line == 1, hit, 0.0)).T
    lane = lax.broadcasted_iota(jnp.int32, (total, 128), 1) // 16
    token = lax.broadcasted_iota(jnp.int32, (total, 128), 0) % 8
    values = jnp.where(lane == token, values, 0.0)
    message[:, :, 1024:1152] = jnp.sum(values.reshape(CHIPS, 8, 128), axis=1, keepdims=True)


def slab_places(meta):
    y, x, c = meta[0], meta[1], meta[2]
    places = []
    for slab in range(SIDE * SIDE):
        row, col = slab // SIDE, slab % SIDE
        step = jnp.where(c == 0, (row - y) % SIDE, (col - x) % SIDE)
        places.append(pl.multiple_of(32 * (SIDE * step + jnp.where(c == 0, col, row)), 32))
    return places


def grad_kernel(
    meta, scaled, spread, scaled_o, spread_o, stats, stats_o, gathered, gathered_o, grad, pair, merged
):
    total, width = grad.shape
    lse, average, live = [], [], []
    token = lax.broadcasted_iota(jnp.int32, (1, 128), 1)
    for k in range(4):
        both = (gathered, gathered_o)
        parts = [part[:, 0, 128 * k : 128 * (k + 1)] for part in both]
        top = jnp.max(jnp.maximum(*parts), axis=0, keepdims=True)
        factors = [jnp.exp(part - top) for part in parts]
        sums = jnp.sum(factors[0] + factors[1], axis=0, keepdims=True)
        lse.append(top + jnp.log(sums))
        moments = [part[:, 0, 512 + 128 * k : 640 + 128 * k] for part in both]
        moment = moments[0] * factors[0] + moments[1] * factors[1]
        average.append(jnp.sum(moment, axis=0, keepdims=True) / sums)
        live.append(jnp.where(token < meta[8 + k], LOSS_SCALE, 0.0))
    lse, average, live = (jnp.concatenate(value, axis=1) for value in (lse, average, live))
    own, far = (live * jnp.exp(top - lse) for top in (stats[0:1, :], stats_o[0:1, :]))
    lines = stack_lines([average, own, far, lse])
    merged[...] = lines[0:8]
    columns = lines.T
    for slab, first in enumerate(slab_places(meta)):
        rows = slice(32 * slab, 32 * slab + 32)
        for side, (e, gap) in enumerate(((scaled, spread), (scaled_o, spread_o))):
            value = (
                columns[rows, side + 1 : side + 2] * e[rows, :] * (gap[rows, :] - columns[rows, 0:1])
            ).astype(bf16)
            if side == 0:
                grad[rows, :] = value
            pair[pl.ds(first, 32), side * width : (side + 1) * width] = value


def params(limit):
    return pltpu.CompilerParams(vmem_limit_bytes=limit)


def cost(flops, moved):
    return pl.CostEstimate(flops=flops, bytes_accessed=moved, transcendentals=0)


def body(teacher_rows, student_rows, teacher_head, student_head, response_ids, lengths, seq_order):
    depth, width = student_head.shape
    half = depth // 2
    total = response_ids.shape[0]
    own = student_rows.shape[0]
    place = lax.axis_index(AXES)
    c, x, y = place % 2, (place // 8) % SIDE, place // 32

    both = jnp.concatenate([student_rows, teacher_rows], axis=0)
    mine = lax.dynamic_slice_in_dim(both, c * half, half, axis=1)
    theirs = swap(lax.dynamic_slice_in_dim(both, (1 - c) * half, half, axis=1))

    def shard(a, b):
        return jnp.where(c == 0, jnp.concatenate([a, b]), jnp.concatenate([b, a]))

    shards = jnp.stack([shard(mine[:own], theirs[:own]), shard(mine[own:], theirs[own:])])
    wide = jnp.broadcast_to(shards[None], (SIDE * SIDE,) + shards.shape)
    wide = lax.all_to_all(wide, AXES, 0, 0, axis_index_groups=PLANES, tiled=True)

    position = jnp.arange(4, dtype=jnp.int32)
    inverse = jnp.sum(jnp.where(seq_order[None, :] == position[:, None], position[None, :], 0), axis=1)
    meta = jnp.concatenate([jnp.stack([y, x, c, place * width]).astype(jnp.int32), inverse, lengths])
    ids = response_ids[:, None]
    far = lax.dynamic_slice_in_dim(student_head, (1 - c) * half, half)
    wide, meta, ids, far = lax.optimization_barrier((wide, meta, ids, far))
    far = swap(far)

    def along_axis(plane, relay=False):
        after, before = (lax.ppermute(plane, AXES, along(step)) for step in (1, 3))
        if relay:
            return [plane, after, before, lax.ppermute(after, AXES, along(1))]
        return [plane, after, before, lax.ppermute(plane, AXES, along(2))]

    student_pieces = along_axis(wide[:, 0].reshape(-1, half))
    teacher_pieces = along_axis(wide[:, 1].reshape(-1, half), True)
    turned = turn_call(meta, student_head, far)
    near = swap(teacher_pieces[0])
    student_pieces, turned, near = lax.optimization_barrier((student_pieces, turned, near))
    student_pieces += [swap(piece) for piece in student_pieces]

    fixed = lambda shape: pl.BlockSpec(shape, lambda n, m: (0,) * len(shape))
    moving = pl.BlockSpec((total, TILE), lambda n, m: (0, n))
    square = jax.ShapeDtypeStruct((total, width), f32)
    line = jax.ShapeDtypeStruct((8, total), f32)
    logits, scaled, stats_s, rows = logits_call(
        STUDENT, student_kernel, meta, student_pieces, student_head, [], [],
        [square, square, line, jax.ShapeDtypeStruct((total, depth), bf16)],
        [fixed((total, width)), fixed((total, width)), fixed((8, total)), pl.BlockSpec(memory_space=pl.ANY)],
        [pltpu.VMEM((total, depth), bf16), pltpu.VMEM((total, 128), f32), pltpu.SemaphoreType.DMA],
    )
    teacher_pieces, stats_s = lax.optimization_barrier((teacher_pieces, stats_s))
    teacher_pieces += [near] + [swap(piece) for piece in teacher_pieces[1:]]
    spread, message = logits_call(
        TEACHER, teacher_kernel, meta, teacher_pieces, teacher_head,
        [logits, scaled, ids, stats_s], [moving, moving, fixed((total, 1)), fixed((8, total))],
        [square, jax.ShapeDtypeStruct((CHIPS, 1, 1152), f32)],
        [moving, fixed((CHIPS, 1, 1152))],
        [pltpu.VMEM((total, depth), bf16), pltpu.VMEM((TILES, total, TILE), f32)]
        + [pltpu.VMEM((total, 128), f32)] * 3,
    )

    gathered = lax.all_to_all(message, AXES, 0, 0, axis_index_groups=CORES, tiled=True)
    scaled, spread, stats_s = lax.optimization_barrier((scaled, spread, stats_s))
    scaled_o, spread_o, stats_o = swap(scaled), swap(spread), swap(stats_s)
    gathered_o = swap(gathered)
    in_vmem = pl.BlockSpec(memory_space=pltpu.VMEM)
    grad, pair, merged = pl.pallas_call(
        grad_kernel,
        in_specs=[pl.BlockSpec(memory_space=pltpu.SMEM)] + [in_vmem] * 8,
        out_specs=[in_vmem] * 3,
        out_shape=[
            jax.ShapeDtypeStruct((total, width), bf16),
            jax.ShapeDtypeStruct((total, 2 * width), bf16),
            jax.ShapeDtypeStruct((8, total), f32),
        ],
        compiler_params=params(SMALL),
        cost_estimate=cost(10 * total * width, 20 * total * width),
    )(meta, scaled, spread, scaled_o, spread_o, stats_s, stats_o, gathered, gathered_o)
    gathered, gathered_o, merged = lax.optimization_barrier((gathered, gathered_o, merged))
    blocks = jnp.dot(pair, turned, preferred_element_type=f32).astype(bf16)
    blocks = blocks.reshape(SIDE, total // SIDE, half)
    kept = blocks[0].astype(f32)
    for step in STEPS[:0:-1]:
        kept = kept + lax.ppermute(blocks[step], AXES, along(SIDE - step)).astype(f32)
    parts = lax.all_to_all(kept.astype(bf16), AXES, 0, 0, axis_index_groups=PLANES, tiled=True)
    head_grad = lax.dot_general(
        rows, grad, (((0,), (0,)), ((), ())), preferred_element_type=f32
    ).astype(bf16)
    mine = jnp.sum(parts.reshape(SIDE * SIDE, 8, half).astype(f32), axis=0).astype(bf16)
    mine, head_grad = lax.optimization_barrier((mine, head_grad))
    keep = lax.dynamic_slice_in_dim(mine, c * own, own)
    take = swap(lax.dynamic_slice_in_dim(mine, (1 - c) * own, own))
    hidden_grad = jnp.where(
        c == 0, jnp.concatenate([keep, take], axis=1), jnp.concatenate([take, keep], axis=1)
    )

    start = place * own
    mine = lax.dynamic_slice_in_dim(merged, start, own, axis=1)
    average, student_lse = mine[0], mine[3]
    teach = jnp.concatenate([gathered[:, 0, 1024:], gathered_o[:, 0, 1024:]]).reshape(2 * CHIPS, 8, 16)
    teach = lax.dynamic_slice_in_dim(teach, c * own, own, axis=1)
    teacher_lse = jax.nn.logsumexp(teach[:, :, 0], axis=0)
    hit = jnp.sum(teach[:, :, 1], axis=0)
    span = total // lengths.shape[0]
    index = start + jnp.arange(own, dtype=jnp.int32)
    live = (index % span < lengths[index // span]).astype(f32)
    token_kl = live * (average - student_lse + teacher_lse)
    sampled_gap = live * (hit - student_lse + teacher_lse)
    return (token_kl, sampled_gap, head_grad, hidden_grad)


def solution(mesh):
    in_specs = (P(AXES, None), P(AXES, None), P(None, AXES), P(None, AXES), P(), P(), P())
    out_specs = (P(AXES), P(AXES), P(None, AXES), P(AXES, None))
    return jax.shard_map(body, mesh=mesh, in_specs=in_specs, out_specs=out_specs, check_vma=False)
```

```python
import jax
import jax.numpy as jnp
from jax import lax
from jax.experimental import pallas as pl
from jax.experimental.pallas import tpu as pltpu
from jax.sharding import PartitionSpec as P

AXES = ("grp", "voc")
LOSS_SCALE = 64.0
SIDE = 4
CHIPS = SIDE**3
LARGE, SMALL = 58 * 1024 * 1024, 44 * 1024 * 1024
STUDENT, TEACHER = 47 * 1024 * 1024, 53 * 1024 * 1024
TILE = 256
TILES = 3
f32 = jnp.float32
bf16 = jnp.bfloat16


def at(y, x, z, c):
    return ((y * SIDE + x) * SIDE + z) * 2 + c


RANGE = range(SIDE)
PLANES = [[at(y, x, z, 0) for x in RANGE for z in RANGE] for y in RANGE] + [
    [at(y, x, z, 1) for y in RANGE for z in RANGE] for x in RANGE
]
CORES = [[2 * chip + c for chip in range(CHIPS)] for c in range(2)]
SWAP = [(i, i ^ 1) for i in range(2 * CHIPS)]
STEPS = (0, 1, 3, 2)


def along(step):
    pairs = []
    for y in RANGE:
        for x in RANGE:
            for z in RANGE:
                pairs.append((at(y, x, z, 0), at((y - step) % SIDE, x, z, 0)))
                pairs.append((at(y, x, z, 1), at(y, (x - step) % SIDE, z, 1)))
    return pairs


def swap(value):
    return lax.ppermute(value, AXES, SWAP)


def assemble(meta, pieces, rows, order):
    y, x, c = meta[0], meta[1], meta[2]
    half = pieces[0].shape[1]
    for index, piece in enumerate(pieces):
        step = STEPS[index % SIDE]
        kind = c if index < SIDE else 1 - c
        for p in range(SIDE):
            row = jnp.where(kind == 0, (y + step) % SIDE, p)
            col = jnp.where(kind == 0, p, (x + step) % SIDE)
            if order is not None:
                row = meta[order + row]
            first = pl.multiple_of((row * SIDE + col) * 32, 32)
            lane = pl.multiple_of(kind * half, half)
            rows[pl.ds(first, 32), pl.ds(lane, half)] = piece[32 * p : 32 * p + 32, :]


def pack(values, rows):
    lane = lax.broadcasted_iota(jnp.int32, (rows, 128), 1)
    packed = jnp.zeros((rows, 128), f32)
    for k, value in enumerate(values):
        packed = jnp.where(lane == k, value, packed)
    return packed


def row_sum(value):
    return jnp.sum(value, axis=1, keepdims=True)


def student_kernel(meta, *refs):
    pieces, (head, logits, scaled, stats, kept, rows, table, sem) = refs[:8], refs[8:]
    n = pl.program_id(0)
    total, width = logits.shape
    tile = head.shape[1]
    save = pltpu.make_async_copy(rows, kept, sem)

    @pl.when(n == 0)
    def _():
        assemble(meta, pieces, rows, None)
        save.start()

    logits[:, pl.ds(pl.multiple_of(n * tile, tile), tile)] = jnp.dot(
        rows[...], head[...], preferred_element_type=f32
    )

    @pl.when(n == pl.num_programs(0) - 1)
    def _():
        chunk = 64
        for i in range(total // chunk):
            here = slice(i * chunk, (i + 1) * chunk)
            s = logits[here, :]
            top = jnp.max(s, axis=1, keepdims=True)
            e = jnp.exp(s - top)
            scaled[here, :] = e
            table[here, :] = pack([top, row_sum(e)], chunk)
        stats[...] = table[...].T[:8]
        save.wait()


def teacher_kernel(meta, *refs):
    pieces, refs = refs[:8], refs[8:]
    head, student, scaled, ids, stats_s, spread, message, rows, teacher, moment, hit, tops = refs
    n = pl.program_id(0)
    total, tile = student.shape
    lanes = 128

    @pl.when(n == 0)
    def _():
        assemble(meta, pieces, rows, 4)
        moment[...] = jnp.zeros_like(moment)
        hit[...] = jnp.zeros_like(hit)
        tops[...] = jnp.full_like(tops, -jnp.inf)

    teacher[n] = jnp.dot(rows[...], head[...], preferred_element_type=f32)
    chunk = 64
    for i in range(total // chunk):
        here = slice(i * chunk, (i + 1) * chunk)
        own = ids[here, :] - meta[3] - n * tile
        for part in range(tile // lanes):
            side = slice(part * lanes, (part + 1) * lanes)
            t = teacher[n, here, side]
            gap = student[here, side] - t
            spread[here, side] = gap
            moment[here, :] += scaled[here, side] * gap
            column = part * lanes + lax.broadcasted_iota(jnp.int32, (chunk, lanes), 1)
            hit[here, :] += jnp.where(column == own, gap, 0.0)
            tops[here, :] = jnp.maximum(tops[here, :], t)

    @pl.when(n == pl.num_programs(0) - 1)
    def _():
        for i in range(total // chunk):
            here = slice(i * chunk, (i + 1) * chunk)
            top = jnp.max(tops[here, :], axis=1, keepdims=True)
            sums = jnp.exp(teacher[0, here, :] - top)
            for k in range(1, TILES):
                sums += jnp.exp(teacher[k, here, :] - top)
            moment[here, :] = pack(
                [row_sum(moment[here, :]), top, row_sum(sums), row_sum(hit[here, :])], chunk
            )
        moments = moment[...].T
        write_message(
            message,
            stats_s[0:1, :] + jnp.log(stats_s[1:2, :]),
            moments[0:1] / stats_s[1:2, :],
            moments[1:2] + jnp.log(moments[2:3]),
            moments[3:4],
        )


def logits_call(limit, kernel, meta, pieces, head, extra, extra_specs, out_shape, out_specs, scratch):
    total, (depth, width) = 4 * pieces[0].shape[0], head.shape
    once = pl.BlockSpec(pieces[0].shape, lambda n, m: (0, 0), pipeline_mode=pl.Buffered(1))
    return pl.pallas_call(
        kernel,
        grid_spec=pltpu.PrefetchScalarGridSpec(
            num_scalar_prefetch=1,
            grid=(TILES,),
            in_specs=[once] * 8 + [pl.BlockSpec((depth, TILE), lambda n, m: (0, n))] + extra_specs,
            out_specs=out_specs,
            scratch_shapes=scratch,
        ),
        out_shape=out_shape,
        compiler_params=params(limit),
        cost_estimate=cost(0, 0),
    )(meta, *pieces, head, *extra)


def turn_kernel(meta, own, far, turned):
    n = pl.program_id(0)
    count = pl.num_programs(0) // 2

    @pl.when(n < count)
    def _():
        turned[...] = own[...].T

    @pl.when(n >= count)
    def _():
        turned[...] = far[...].T


def turn_call(meta, head, far):
    half, width = far.shape
    block = 512
    count = half // block
    return pl.pallas_call(
        turn_kernel,
        grid_spec=pltpu.PrefetchScalarGridSpec(
            num_scalar_prefetch=1,
            grid=(2 * count,),
            in_specs=[
                pl.BlockSpec((block, width), lambda n, m: (m[2] * count + jnp.minimum(n, count - 1), 0)),
                pl.BlockSpec((block, width), lambda n, m: (jnp.maximum(n - count, 0), 0)),
            ],
            out_specs=pl.BlockSpec((width, block), lambda n, m: (n // count, n % count)),
        ),
        out_shape=jax.ShapeDtypeStruct((2 * width, half), bf16),
        compiler_params=params(LARGE),
        cost_estimate=cost(0, 8 * half * width),
    )(meta, head, far)


def stack_lines(values):
    line = lax.broadcasted_iota(jnp.int32, (128, values[0].shape[1]), 0)
    lines = jnp.zeros((128, values[0].shape[1]), f32)
    for k, value in enumerate(values):
        lines = jnp.where(line == k, value, lines)
    return lines


def write_message(message, lse, average, lse_t, hit):
    total = lse.shape[1]
    for k in range(4):
        here = slice(128 * k, 128 * (k + 1))
        for base, value in ((0, lse), (4, average)):
            lanes = slice(128 * (base + k), 128 * (base + k + 1))
            message[:, :, lanes] = jnp.broadcast_to(value[:, here].reshape(1, 1, 128), (CHIPS, 1, 128))
    line = lax.broadcasted_iota(jnp.int32, (128, total), 0) % 16
    values = jnp.where(line == 0, lse_t, jnp.where(line == 1, hit, 0.0)).T
    lane = lax.broadcasted_iota(jnp.int32, (total, 128), 1) // 16
    token = lax.broadcasted_iota(jnp.int32, (total, 128), 0) % 8
    values = jnp.where(lane == token, values, 0.0)
    message[:, :, 1024:1152] = jnp.sum(values.reshape(CHIPS, 8, 128), axis=1, keepdims=True)


def slab_places(meta):
    y, x, c = meta[0], meta[1], meta[2]
    places = []
    for slab in range(SIDE * SIDE):
        row, col = slab // SIDE, slab % SIDE
        step = jnp.where(c == 0, (row - y) % SIDE, (col - x) % SIDE)
        places.append(pl.multiple_of(32 * (SIDE * step + jnp.where(c == 0, col, row)), 32))
    return places


def grad_kernel(
    meta, scaled, spread, scaled_o, spread_o, stats, stats_o, gathered, gathered_o, grad, pair, merged
):
    total, width = grad.shape
    lse, average, live = [], [], []
    token = lax.broadcasted_iota(jnp.int32, (1, 128), 1)
    for k in range(4):
        both = (gathered, gathered_o)
        parts = [part[:, 0, 128 * k : 128 * (k + 1)] for part in both]
        top = jnp.max(jnp.maximum(*parts), axis=0, keepdims=True)
        factors = [jnp.exp(part - top) for part in parts]
        sums = jnp.sum(factors[0] + factors[1], axis=0, keepdims=True)
        lse.append(top + jnp.log(sums))
        moments = [part[:, 0, 512 + 128 * k : 640 + 128 * k] for part in both]
        moment = moments[0] * factors[0] + moments[1] * factors[1]
        average.append(jnp.sum(moment, axis=0, keepdims=True) / sums)
        live.append(jnp.where(token < meta[8 + k], LOSS_SCALE, 0.0))
    lse, average, live = (jnp.concatenate(value, axis=1) for value in (lse, average, live))
    own, far = (live * jnp.exp(top - lse) for top in (stats[0:1, :], stats_o[0:1, :]))
    lines = stack_lines([average, own, far, lse])
    merged[...] = lines[0:8]
    columns = lines.T
    for slab, first in enumerate(slab_places(meta)):
        rows = slice(32 * slab, 32 * slab + 32)
        for side, (e, gap) in enumerate(((scaled, spread), (scaled_o, spread_o))):
            value = (
                columns[rows, side + 1 : side + 2] * e[rows, :] * (gap[rows, :] - columns[rows, 0:1])
            ).astype(bf16)
            if side == 0:
                grad[rows, :] = value
            pair[pl.ds(first, 32), side * width : (side + 1) * width] = value


def params(limit):
    return pltpu.CompilerParams(vmem_limit_bytes=limit)


def cost(flops, moved):
    return pl.CostEstimate(flops=flops, bytes_accessed=moved, transcendentals=0)


def body(teacher_rows, student_rows, teacher_head, student_head, response_ids, lengths, seq_order):
    depth, width = student_head.shape
    half = depth // 2
    total = response_ids.shape[0]
    own = student_rows.shape[0]
    place = lax.axis_index(AXES)
    c, x, y = place % 2, (place // 8) % SIDE, place // 32

    both = jnp.concatenate([student_rows, teacher_rows], axis=0)
    mine = lax.dynamic_slice_in_dim(both, c * half, half, axis=1)
    theirs = swap(lax.dynamic_slice_in_dim(both, (1 - c) * half, half, axis=1))

    def shard(a, b):
        return jnp.where(c == 0, jnp.concatenate([a, b]), jnp.concatenate([b, a]))

    shards = jnp.stack([shard(mine[:own], theirs[:own]), shard(mine[own:], theirs[own:])])
    wide = jnp.broadcast_to(shards[None], (SIDE * SIDE,) + shards.shape)
    wide = lax.all_to_all(wide, AXES, 0, 0, axis_index_groups=PLANES, tiled=True)

    position = jnp.arange(4, dtype=jnp.int32)
    inverse = jnp.sum(jnp.where(seq_order[None, :] == position[:, None], position[None, :], 0), axis=1)
    meta = jnp.concatenate([jnp.stack([y, x, c, place * width]).astype(jnp.int32), inverse, lengths])
    ids = response_ids[:, None]
    far = lax.dynamic_slice_in_dim(student_head, (1 - c) * half, half)
    wide, meta, ids, far = lax.optimization_barrier((wide, meta, ids, far))
    far = swap(far)

    def along_axis(plane, relay=False):
        after, before = (lax.ppermute(plane, AXES, along(step)) for step in (1, 3))
        if relay:
            return [plane, after, before, lax.ppermute(after, AXES, along(1))]
        return [plane, after, before, lax.ppermute(plane, AXES, along(2))]

    student_pieces = along_axis(wide[:, 0].reshape(-1, half))
    teacher_pieces = along_axis(wide[:, 1].reshape(-1, half), True)
    turned = turn_call(meta, student_head, far)
    near = swap(teacher_pieces[0])
    student_pieces, turned, near = lax.optimization_barrier((student_pieces, turned, near))
    student_pieces += [swap(piece) for piece in student_pieces]

    fixed = lambda shape: pl.BlockSpec(shape, lambda n, m: (0,) * len(shape))
    moving = pl.BlockSpec((total, TILE), lambda n, m: (0, n))
    square = jax.ShapeDtypeStruct((total, width), f32)
    line = jax.ShapeDtypeStruct((8, total), f32)
    logits, scaled, stats_s, rows = logits_call(
        STUDENT, student_kernel, meta, student_pieces, student_head, [], [],
        [square, square, line, jax.ShapeDtypeStruct((total, depth), bf16)],
        [fixed((total, width)), fixed((total, width)), fixed((8, total)), pl.BlockSpec(memory_space=pl.ANY)],
        [pltpu.VMEM((total, depth), bf16), pltpu.VMEM((total, 128), f32), pltpu.SemaphoreType.DMA],
    )
    teacher_pieces, stats_s = lax.optimization_barrier((teacher_pieces, stats_s))
    teacher_pieces += [near] + [swap(piece) for piece in teacher_pieces[1:]]
    spread, message = logits_call(
        TEACHER, teacher_kernel, meta, teacher_pieces, teacher_head,
        [logits, scaled, ids, stats_s], [moving, moving, fixed((total, 1)), fixed((8, total))],
        [square, jax.ShapeDtypeStruct((CHIPS, 1, 1152), f32)],
        [moving, fixed((CHIPS, 1, 1152))],
        [pltpu.VMEM((total, depth), bf16), pltpu.VMEM((TILES, total, TILE), f32)]
        + [pltpu.VMEM((total, 128), f32)] * 3,
    )

    gathered = lax.all_to_all(message, AXES, 0, 0, axis_index_groups=CORES, tiled=True)
    scaled, spread, stats_s = lax.optimization_barrier((scaled, spread, stats_s))
    scaled_o, spread_o, stats_o = swap(scaled), swap(spread), swap(stats_s)
    gathered_o = swap(gathered)
    in_vmem = pl.BlockSpec(memory_space=pltpu.VMEM)
    grad, pair, merged = pl.pallas_call(
        grad_kernel,
        in_specs=[pl.BlockSpec(memory_space=pltpu.SMEM)] + [in_vmem] * 8,
        out_specs=[in_vmem] * 3,
        out_shape=[
            jax.ShapeDtypeStruct((total, width), bf16),
            jax.ShapeDtypeStruct((total, 2 * width), bf16),
            jax.ShapeDtypeStruct((8, total), f32),
        ],
        compiler_params=params(SMALL),
        cost_estimate=cost(10 * total * width, 20 * total * width),
    )(meta, scaled, spread, scaled_o, spread_o, stats_s, stats_o, gathered, gathered_o)
    gathered, gathered_o, merged = lax.optimization_barrier((gathered, gathered_o, merged))
    blocks = jnp.dot(pair, turned, preferred_element_type=f32).astype(bf16)
    blocks = blocks.reshape(SIDE, total // SIDE, half)
    kept = blocks[0].astype(f32)
    for step in STEPS[:0:-1]:
        kept = kept + lax.ppermute(blocks[step], AXES, along(SIDE - step)).astype(f32)
    parts = lax.all_to_all(kept.astype(bf16), AXES, 0, 0, axis_index_groups=PLANES, tiled=True)
    head_grad = lax.dot_general(
        rows, grad, (((0,), (0,)), ((), ())), preferred_element_type=f32
    ).astype(bf16)
    mine = jnp.sum(parts.reshape(SIDE * SIDE, 8, half).astype(f32), axis=0).astype(bf16)
    mine, head_grad = lax.optimization_barrier((mine, head_grad))
    keep = lax.dynamic_slice_in_dim(mine, c * own, own)
    take = swap(lax.dynamic_slice_in_dim(mine, (1 - c) * own, own))
    hidden_grad = jnp.where(
        c == 0, jnp.concatenate([keep, take], axis=1), jnp.concatenate([take, keep], axis=1)
    )

    start = place * own
    mine = lax.dynamic_slice_in_dim(merged, start, own, axis=1)
    average, student_lse = mine[0], mine[3]
    teach = jnp.concatenate([gathered[:, 0, 1024:], gathered_o[:, 0, 1024:]]).reshape(2 * CHIPS, 8, 16)
    teach = lax.dynamic_slice_in_dim(teach, c * own, own, axis=1)
    teacher_lse = jax.nn.logsumexp(teach[:, :, 0], axis=0)
    hit = jnp.sum(teach[:, :, 1], axis=0)
    span = total // lengths.shape[0]
    index = start + jnp.arange(own, dtype=jnp.int32)
    live = (index % span < lengths[index // span]).astype(f32)
    token_kl = live * (average - student_lse + teacher_lse)
    sampled_gap = live * (hit - student_lse + teacher_lse)
    return (token_kl, sampled_gap, head_grad, hidden_grad)


def solution(mesh):
    in_specs = (P(AXES, None), P(AXES, None), P(None, AXES), P(None, AXES), P(), P(), P())
    out_specs = (P(AXES), P(AXES), P(None, AXES), P(AXES, None))
    return jax.shard_map(body, mesh=mesh, in_specs=in_specs, out_specs=out_specs, check_vma=False)
```
